256 devices in a mesh: dp: 4 (over x_lo, core), context: 16 (over x_hi, z), expert: 4 (over y).
Axes of the slice: x: 4 (x_hi: 2, x_lo: 2; x = x_hi * 2 + x_lo), y: 4, z: 8, core: 2. Of those that a mesh axis runs over, the one named last changes fastest.
Arguments:
- inputs: bfloat16 [16, 2048, 1024], P(('dp', 'expert'), 'context'), may hold values from -6 to 6
- cotangent: bfloat16 [16, 2048, 1024], P(('dp', 'expert'), 'context'), may hold values from -6 to 6
- doc_lengths: int32 [16, 8], P(('dp', 'expert')), may hold values from 1 to 1024, 2048 in all within a row
- choices: int32 [16, 2048, 8], P(('dp', 'expert'), 'context'), may hold values from 0 to 15, all different within a row; in each aligned block of 128 rows (0 to 127, 128 to 255, ..., all dimensions but the last counted through in order) at most 96 rows name the same one
- first_gain: float32 [1024], replicated, may hold values from 0.5 to 1.5
- query_weight: bfloat16 [1024, 1024], replicated, may hold values from -0.25 to 0.25
- key_weight: bfloat16 [1024, 512], replicated, may hold values from -0.25 to 0.25
- value_weight: bfloat16 [1024, 512], replicated, may hold values from -0.1875 to 0.1875
- out_weight: bfloat16 [1024, 1024], replicated, may hold values from -0.75 to 0.75
- second_gain: float32 [1024], replicated, may hold values from 0.5 to 1.5
- router_weight: bfloat16 [1024, 16], replicated, may hold values from -0.08984375 to 0.08984375
- gate_weight: bfloat16 [16, 1024, 512], P('expert'), may hold values from -0.1875 to 0.1875
- up_weight: bfloat16 [16, 1024, 512], P('expert'), may hold values from -0.1875 to 0.1875
- down_weight: bfloat16 [16, 512, 1024], P('expert'), may hold values from -1 to 1
Outputs:
- outputs: bfloat16 [16, 2048, 1024], P(('dp', 'expert'), 'context')
- grad_inputs: bfloat16 [16, 2048, 1024], P(('dp', 'expert'), 'context')
- grad_first_gain: float32 [1024], P(('dp', 'context', 'expert'))
- grad_query_weight: float32 [1024, 1024], P(('dp', 'context', 'expert'))
- grad_key_weight: float32 [1024, 512], P(('dp', 'context', 'expert'))
- grad_value_weight: float32 [1024, 512], P(('dp', 'context', 'expert'))
- grad_out_weight: float32 [1024, 1024], P(('dp', 'context', 'expert'))
- grad_second_gain: float32 [1024], P(('dp', 'context', 'expert'))
- grad_router_weight: float32 [1024, 16], P(('dp', 'context', 'expert'))
- grad_gate_weight: float32 [16, 1024, 512], P('expert', ('dp', 'context'))
- grad_up_weight: float32 [16, 1024, 512], P('expert', ('dp', 'context'))
- grad_down_weight: float32 [16, 512, 1024], P('expert', ('dp', 'context'))
The draws below stay inside these ranges and needn't reach their ends.
Inputs may be any that keep to these rules, and one draw needn't show every extreme that they name: `doc_lengths`: each sequence's 8 documents fill its 2048 positions in order, and one of them has exactly 1024 tokens. `choices`: each token names 8 different experts. Among the rows of one device no expert is named more than 96 times, and in every draw some device names some expert exactly 96 times.
All inputs are finite; a program needn't handle non-finite values.
Results may differ from the reference program's by a relative error of at most 0.035.
Values may be sent and summed in bfloat16 or wider, within the bound.
No kernel may reach another device: no remote copies, remote signals or barrier semaphores. Data moves between devices by JAX's collectives and lax.ppermute only.
A program may use at most 192 MiB of HBM per device.

```python
import math
import jax
import jax.numpy as jnp
import numpy as np
from jax import lax

D = 1024
HEADS = 16
KV_HEADS = 8
HEAD_DIM = 64
EXPERT_FF = 512
TOP = 8
DOCS = 8
DOC_MOST = 1024
LENGTH = 2048
DEV_TOKENS = 128
SEQUENCES = 16
EXPERTS = 16
CAPACITY = 96


def shard_levels(rng, shape, cuts, least, largest):
    factor_of = 1.0
    for axis_at, shards_of in cuts:
        steps = jax.random.uniform(jax.random.fold_in(jax.random.fold_in(rng, 6), axis_at), (shards_of,), jnp.float32, least / len(cuts), largest / len(cuts))
        factor_of = factor_of * jnp.repeat(jnp.exp(steps), shape[axis_at] // shards_of).reshape((-1,) + (1,) * (len(shape) - 1 - axis_at))
    return factor_of


def profile(count, total, bound, skew):
    weights = [(1 << 20) // math.isqrt(rank ** skew) + 1 for rank in range(2, count + 1)]
    spare, counts = total - bound - (count - 1), [1] * (count - 1)
    while spare > 0:
        free = [i for i in range(count - 1) if counts[i] < bound]
        mass, remaining = sum([weights[i] for i in free]), spare
        for i in free:
            more = min(bound - counts[i], max(1, remaining * weights[i] // mass), spare)
            counts[i] = counts[i] + more
            spare = spare - more
    return np.array([bound] + counts)


def uneven_parts(own_key, number_of, total, most, skew):
    if number_of == 2:
        one = jax.random.randint(own_key, (), max(1, total - most), min(most, total - 1) + 1)
        return jnp.stack([one, total - one])
    tallies = jnp.asarray(profile(number_of, total, most, skew), jnp.int32)
    pairs = (number_of - 1) // 2
    donor, taker = tallies[1:1 + 2 * pairs:2], tallies[2:2 + 2 * pairs:2]
    room = jnp.minimum(donor - 1, most - taker)
    passed = jax.random.randint(jax.random.fold_in(own_key, 1), (pairs,), 0, 1 << 20) % (room + 1)
    tallies = tallies.at[1:1 + 2 * pairs:2].set(donor - passed).at[2:2 + 2 * pairs:2].set(taker + passed)
    return tallies[jax.random.permutation(jax.random.fold_in(own_key, 2), number_of)]


def routed_block(rng, own, number, rows, amount, top, reach, slope):
    ranking = jax.random.permutation(rng, amount)
    heavy_load, usual = load_shares(amount, rows * top, reach, slope, True), load_shares(amount, rows * top, reach, slope, False)
    places = jnp.arange(amount)

    def named(sizes, rotation):
        used = int((sizes > 0).sum())
        fixed = max(1, used // 4)
        moved = fixed + (places - fixed + rotation * (used - fixed)) % max(1, amount - fixed)
        return jnp.zeros((amount,), jnp.int32).at[ranking[jnp.where(places < fixed, places, moved)]].set(jnp.asarray(sizes, jnp.int32))

    sizes = jnp.where(number % 4 == 0, named(heavy_load, number // 4), named(usual, number - number // 4 - 1))
    mixed = jax.random.permutation(jax.random.fold_in(own, 3), amount)
    source_of, receiver = mixed[0:amount // 2 * 2:2], mixed[1:amount // 2 * 2:2]
    margin = jnp.minimum(sizes[source_of] - 1, reach - sizes[receiver]) // 2
    margin = jnp.where((source_of == ranking[0]) | (receiver == ranking[0]) | (sizes[receiver] == 0), 0, jnp.maximum(margin, 0))
    moved = jax.random.randint(jax.random.fold_in(own, 4), (amount // 2,), 0, 1 << 20) % (margin + 1)
    sizes = sizes.at[source_of].add(-moved).at[receiver].add(moved)
    labels = jnp.searchsorted(jnp.cumsum(sizes), jnp.arange(rows * top), side="right").astype(jnp.int32)
    grid = labels.reshape(top, rows).T
    grid = grid[jax.random.permutation(jax.random.fold_in(own, 1), rows)]
    rotation = jax.random.randint(jax.random.fold_in(own, 2), (rows, 1), 0, top)
    return jnp.take_along_axis(grid, (jnp.arange(top)[None, :] + rotation) % top, axis=1)


def load_shares(count, total, limit, slope, full):
    loads = [(1 << 20) // math.isqrt(standing ** slope) + 1 for standing in range(1, count + 1)]
    largest = limit if full else min(limit, max(-(-total // count), total * loads[0] // sum(loads)))
    least = 1 if total - largest >= count - 1 else 0
    holding, spare = [largest] + [least] * (count - 1), total - largest - least * (count - 1)
    while spare > 0:
        free = [i for i in range(1, count) if holding[i] < largest] or [i for i in range(1, count) if holding[i] < limit]
        whole, left = sum([loads[i] for i in free]), spare
        for i in free:
            more = min(limit - holding[i], max(1, left * loads[i] // whole), spare)
            holding[i] = holding[i] + more
            spare = spare - more
    return np.array(holding)


def centred(own_key, dims, spread, most, cuts=(), kind=jnp.bfloat16):
    drawn = jax.random.normal(own_key, dims, jnp.float32) * spread
    if len(cuts) > 0:
        drawn = shard_levels(own_key, dims, cuts, -0.22, 0.18) * drawn
    return jnp.clip(drawn, min=-most, max=most).astype(kind)


def setup_inputs(seed: int = 0) -> dict:
    key_of = jax.random.split(jax.random.key(seed), 15)
    inputs = centred(key_of[0], (SEQUENCES, LENGTH, D), 1.0, 6.0, ((0, 16), (1, 16)))
    cotangent = centred(key_of[1], (SEQUENCES, LENGTH, D), 1.0, 6.0, ((0, 16), (1, 16)))
    doc_lengths = jax.vmap(lambda own: uneven_parts(own, DOCS, LENGTH, DOC_MOST, 2))(jax.random.split(key_of[2], SEQUENCES)).reshape((SEQUENCES, DOCS)).astype(jnp.int32)
    choices_keys = jax.random.split(jax.random.fold_in(key_of[3], 1), SEQUENCES * LENGTH // DEV_TOKENS)
    choices_turns = jax.random.permutation(jax.random.fold_in(key_of[3], 3), SEQUENCES * LENGTH // DEV_TOKENS)
    choices = jax.vmap(lambda own, number: routed_block(jax.random.fold_in(key_of[3], 2), own, number, DEV_TOKENS, EXPERTS, TOP, CAPACITY, 1))(choices_keys, choices_turns).reshape((SEQUENCES, LENGTH, TOP))
    first_gain = jnp.clip(1.0 + 0.1 * jax.random.normal(key_of[4], (D,), jnp.float32), 0.5, 1.5)
    query_weight = centred(key_of[5], (D, HEADS * HEAD_DIM), (D // 2) ** -0.5, 0.25)
    key_weight = centred(key_of[6], (D, KV_HEADS * HEAD_DIM), (D // 2) ** -0.5, 0.25)
    value_weight = centred(key_of[7], (D, KV_HEADS * HEAD_DIM), D ** -0.5, 0.1875)
    out_weight = centred(key_of[8], (HEADS * HEAD_DIM, D), (HEADS * HEAD_DIM // 16) ** -0.5, 0.75)
    second_gain = jnp.clip(1.0 + 0.1 * jax.random.normal(key_of[9], (D,), jnp.float32), 0.5, 1.5)
    router_weight = centred(key_of[10], (D, EXPERTS), 0.015625, 0.08984375)
    gate_weight = centred(key_of[11], (EXPERTS, D, EXPERT_FF), D ** -0.5, 0.1875, ((0, 4),))
    up_weight = centred(key_of[12], (EXPERTS, D, EXPERT_FF), D ** -0.5, 0.1875, ((0, 4),))
    down_weight = centred(key_of[13], (EXPERTS, EXPERT_FF, D), (EXPERT_FF // 16) ** -0.5, 1.0, ((0, 4),))
    return {"inputs": inputs, "cotangent": cotangent, "doc_lengths": doc_lengths, "choices": choices, "first_gain": first_gain, "query_weight": query_weight, "key_weight": key_weight, "value_weight": value_weight, "out_weight": out_weight, "second_gain": second_gain, "router_weight": router_weight, "gate_weight": gate_weight, "up_weight": up_weight, "down_weight": down_weight}


EPSILON = 1e-06
THETA = 10000.0
NEGATIVE = -1e+30
HIGHEST = lax.Precision.HIGHEST

@jax.custom_vjp
def low(v):
    return lax.optimization_barrier(v.astype(jnp.bfloat16)).astype(jnp.float32)

@jax.custom_vjp
def low_back(v):
    return v

def low_keep(v):
    return (low(v), None)

def low_pass(kept, grad):
    return (grad,)

def back_keep(v):
    return (v, None)

def back_low(kept, grad):
    return (low(grad),)
low.defvjp(low_keep, low_pass)
low_back.defvjp(back_keep, back_low)

def matmul(left, right):
    return jnp.dot(left, right, precision=HIGHEST, preferred_element_type=jnp.float32)

def norm_rows(values_in, gain_vector):
    inverse = lax.rsqrt(lax.optimization_barrier(jnp.mean(values_in * values_in, axis=1, keepdims=True)) + EPSILON)
    return values_in * inverse * gain_vector

def turn_heads(values_in, places, direction):
    halfway = values_in.shape[-1] // 2
    frequency = THETA ** (-jnp.arange(halfway, dtype=jnp.float32) * 2.0 / values_in.shape[-1])
    angles = places[:, None] * frequency[None, :]
    cosine = jnp.cos(angles)[:, None, :]
    sine_part = direction * jnp.sin(angles)[:, None, :]
    former = values_in[..., :halfway]
    latter = values_in[..., halfway:]
    return jnp.concatenate([former * cosine - latter * sine_part, latter * cosine + former * sine_part], axis=-1)

def sequence_forward(parameters, source, lengths_row, chosen_rows):
    first_gain, query_weight, key_weight, value_weight, out_weight, second_gain, router_weight, gate_weight, up_weight, down_weight = parameters
    group_size = HEADS // KV_HEADS
    score_scale = HEAD_DIM ** (-0.5)
    positions = jnp.arange(LENGTH, dtype=jnp.int32)
    starts = jnp.cumsum(lengths_row, dtype=jnp.int32) - lengths_row
    begins = lax.optimization_barrier(jnp.max(jnp.where(starts[None, :] <= positions[:, None], starts[None, :], 0), axis=1))
    relative = (positions - begins).astype(jnp.float32)
    normed_one = low(norm_rows(source, first_gain))
    queries = low(turn_heads(low_back(matmul(normed_one, query_weight)).reshape(LENGTH, HEADS, HEAD_DIM), relative, 1.0))
    queries = queries.reshape(LENGTH, KV_HEADS, group_size, HEAD_DIM)
    key_rows = low(turn_heads(low_back(matmul(normed_one, key_weight)).reshape(LENGTH, KV_HEADS, HEAD_DIM), relative, 1.0))
    value_rows = low(low_back(matmul(normed_one, value_weight))).reshape(LENGTH, KV_HEADS, HEAD_DIM)
    block_size = min(512, LENGTH)

    def attend(block_index):
        first_row = block_index * block_size
        block_queries = lax.dynamic_slice_in_dim(queries, first_row, block_size, 0)
        block_places = lax.dynamic_slice_in_dim(positions, first_row, block_size, 0)
        block_begins = lax.dynamic_slice_in_dim(begins, first_row, block_size, 0)
        allowed = (positions[None, :] <= block_places[:, None]) & (positions[None, :] >= block_begins[:, None])
        scores = low_back(jnp.einsum('qhgd,khd->hgqk', block_queries, key_rows, precision=HIGHEST) * score_scale)
        scores = jnp.where(allowed, scores, NEGATIVE)
        row_top = lax.optimization_barrier(jnp.max(scores, axis=-1, keepdims=True))
        weights = jnp.where(allowed, jnp.exp(scores - row_top), 0.0)
        probabilities = low(weights / lax.optimization_barrier(jnp.sum(weights, axis=-1, keepdims=True)))
        mixed_heads = jnp.einsum('hgqk,khd->qhgd', probabilities, value_rows, precision=HIGHEST)
        return mixed_heads.reshape(block_size, HEADS * HEAD_DIM)
    mixed_all = lax.map(jax.checkpoint(attend), jnp.arange(LENGTH // block_size, dtype=jnp.int32))
    mix_low = low_back(low(mixed_all.reshape(LENGTH, HEADS * HEAD_DIM)))
    residual = source + low_back(matmul(mix_low, out_weight))
    normed_two = low(norm_rows(residual, second_gain))
    logits = matmul(normed_two, router_weight)
    onehot = (chosen_rows[:, :, None] == jnp.arange(EXPERTS, dtype=jnp.int32)).astype(jnp.float32)
    gate_values = jax.nn.softmax(lax.optimization_barrier(jnp.sum(onehot * logits[:, None, :], axis=2)), axis=1)
    dense_gates = lax.optimization_barrier(jnp.sum(gate_values[:, :, None] * onehot, axis=1))

    def expert_step(running_total, expert_index):
        routed_rows = low_back(normed_two)
        gate_pre = low_back(matmul(routed_rows, gate_weight[expert_index]))
        up_pre = low_back(matmul(routed_rows, up_weight[expert_index]))
        activated = low(jax.nn.silu(gate_pre) * up_pre)
        produced = low_back(low(matmul(activated, down_weight[expert_index])))
        return (running_total + produced * dense_gates[:, expert_index][:, None], None)
    expert_sum, unused = lax.scan(jax.checkpoint(expert_step), jnp.zeros_like(source), jnp.arange(EXPERTS, dtype=jnp.int32))
    return residual + expert_sum

def reference(inputs, cotangent, doc_lengths, choices, first_gain, query_weight, key_weight, value_weight, out_weight, second_gain, router_weight, gate_weight, up_weight, down_weight):
    parameters = tuple((argument_array.astype(jnp.float32) for argument_array in (first_gain, query_weight, key_weight, value_weight, out_weight, second_gain, router_weight, gate_weight, up_weight, down_weight)))
    sources = inputs.astype(jnp.float32)

    def whole_layer(layer_parameters, layer_sources):

        def per_sequence(carry_value, sequence_item):
            source, lengths_row, chosen_rows = sequence_item
            return (carry_value, jax.checkpoint(sequence_forward)(layer_parameters, source, lengths_row, chosen_rows))
        unused, results = lax.scan(per_sequence, jnp.zeros((), jnp.float32), (layer_sources, doc_lengths, choices))
        return results
    results, pullback = jax.vjp(whole_layer, parameters, sources)
    param_grads, source_grads = pullback(cotangent.astype(jnp.float32))
    return (results.astype(jnp.bfloat16), source_grads.astype(jnp.bfloat16), param_grads[0], param_grads[1], param_grads[2], param_grads[3], param_grads[4], param_grads[5], param_grads[6], param_grads[7], param_grads[8], param_grads[9])
```

```python
import functools

import jax
import jax.numpy as jnp
from jax import lax
from jax.experimental import pallas as pl
from jax.experimental.pallas import tpu as pltpu
from jax.sharding import PartitionSpec as P

HEADS = 16
KV_HEADS = 8
HEAD_DIM = 64
TOP = 8
EPSILON = 1e-06
THETA = 10000.0
NEGATIVE = -1e30
SCALE = HEAD_DIM ** (-0.5)
BF16 = jnp.bfloat16
F32 = jnp.float32
ROWS = 128
LANES = 128
Z = 8
HALF = Z * ROWS
STEP = 256
PART = 256
PAIRS = KV_HEADS // 2
VMEM_LIMIT = 60 * 1024 * 1024

NN = (((1,), (0,)), ((), ()))
NT = (((1,), (1,)), ((), ()))
TN = (((0,), (0,)), ((), ()))


def dot(left, right, dims=NN):
    return lax.dot_general(left, right, dims, preferred_element_type=F32)


def lanes_of(value):
    return lax.broadcasted_iota(jnp.int32, value.shape, 1)


def swap_halves(value):
    return jnp.where(
        lanes_of(value) % 64 < 32, pltpu.roll(value, 96, 1), pltpu.roll(value, 32, 1)
    )


def exchange(first, second):
    low = lanes_of(first) < 64
    return (
        jnp.where(low, first, pltpu.roll(second, 64, 1)),
        jnp.where(low, pltpu.roll(first, 64, 1), second),
    )


def stack_heads(tile):
    low = lanes_of(tile) < 64
    return jnp.concatenate([jnp.where(low, tile, 0.0), jnp.where(low, 0.0, tile)], axis=0)


def unstack_heads(stacked):
    rows = stacked.shape[0] // 2
    return jnp.where(lanes_of(stacked[:rows]) < 64, stacked[:rows], stacked[rows:])


def turn(tile, cos, sin):
    return tile * cos + swap_halves(tile) * sin


def params():
    return pltpu.CompilerParams(vmem_limit_bytes=VMEM_LIMIT)


def whole(shape):
    return pl.BlockSpec(shape, lambda *_: (0,) * len(shape))


def column(rows, width):
    return pl.BlockSpec((rows, width), lambda j: (0, j))


def cost(microseconds):
    return pl.CostEstimate(
        flops=int(microseconds * 1.1e9),
        bytes_accessed=int(microseconds * 3.6e6),
        transcendentals=0,
    )


def held(values):
    return lax.optimization_barrier(values)


def project_kernel(
    src_ref, gain_ref, wq_ref, wk_ref, wv_ref, cos_ref, sin_ref, normed_ref, out_ref
):
    @pl.when(pl.program_id(0) == 0)
    def _():
        source = src_ref[...].astype(F32)
        inverse = lax.rsqrt(jnp.mean(source * source, axis=1, keepdims=True) + EPSILON)
        normed_ref[...] = (source * inverse * gain_ref[...]).astype(BF16)

    normed = normed_ref[...]
    cos = cos_ref[...]
    sin = sin_ref[...]
    queries = dot(normed, wq_ref[...])
    keys = turn(dot(normed, wk_ref[...]), cos, sin)
    values = dot(normed, wv_ref[...])
    for which, pair in enumerate(exchange(keys, values)):
        tile = queries[:, which * LANES : (which + 1) * LANES]
        out_ref[which, :, :LANES] = (turn(tile, cos, sin) * SCALE).astype(BF16)
        out_ref[which, :, LANES:] = pair.astype(BF16)


def project(source, gain, query_weight, key_weight, value_weight, cos, sin):
    rows, width = source.shape
    return pl.pallas_call(
        project_kernel,
        grid=(PAIRS,),
        in_specs=[
            whole((rows, width)),
            whole((1, width)),
            column(width, 2 * LANES),
            column(width, LANES),
            column(width, LANES),
            whole((rows, LANES)),
            whole((rows, LANES)),
        ],
        out_specs=[
            whole((rows, width)),
            pl.BlockSpec((2, rows, 2 * LANES), lambda j: (j, 0, 0)),
        ],
        out_shape=[
            jax.ShapeDtypeStruct((rows, width), BF16),
            jax.ShapeDtypeStruct((Z, rows, 2 * LANES), BF16),
        ],
        compiler_params=params(),
        cost_estimate=cost(5),
        name="project",
    )(source, gain, query_weight, key_weight, value_weight, cos, sin)


def fill_keys(half_ref, heads_ref, peer_ref, keys, values):
    own = jnp.concatenate([heads_ref[z, :, LANES:] for z in range(Z)], axis=0)
    for tile, start in ((peer_ref[...], 0), (own, pl.multiple_of(half_ref[0] * HALF, HALF))):
        tile = tile.astype(F32)
        low = lanes_of(tile) < 64
        other = pltpu.roll(tile, 64, 1)
        keys[pl.ds(start, HALF), :] = jnp.where(low, tile, other).astype(BF16)
        values[pl.ds(start, HALF), :] = jnp.where(low, other, tile).astype(BF16)


def step_queries(heads_ref, i):
    tiles = [heads_ref[i * (STEP // ROWS) + s, :, :LANES] for s in range(STEP // ROWS)]
    return stack_heads(jnp.concatenate(tiles, axis=0).astype(F32)).astype(BF16)


def step_scores(keys, queries, block, place, last):
    at = pl.ds(pl.multiple_of(block * STEP, STEP), STEP)
    scores = dot(keys[at, :], queries, NT)
    back = last - (block * STEP + lax.broadcasted_iota(jnp.int32, scores.shape, 0))
    return at, jnp.where((back >= 0) & (back <= place), scores, NEGATIVE)


def attend_kernel(
    half_ref, heads_ref, peer_ref, place_ref, mix_ref, out_ref, lse_ref, keys, values, kept
):
    i = pl.program_id(0)

    @pl.when(i == 0)
    def _():
        fill_keys(half_ref, heads_ref, peer_ref, keys, values)

    queries = step_queries(heads_ref, i)
    place = place_ref[0]
    diagonal = half_ref[0] * (HALF // STEP) + i
    first = half_ref[1 + i]
    last = diagonal * STEP + lax.broadcasted_iota(jnp.int32, place.shape, 1) % STEP

    def score(block, top):
        _, scores = step_scores(keys, queries, block, place, last)
        kept[pl.ds(pl.multiple_of((block - first) * STEP, STEP), STEP), :] = scores
        return jnp.maximum(top, jnp.max(scores, axis=0, keepdims=True))

    top = lax.fori_loop(first, diagonal + 1, score, jnp.full(place.shape, NEGATIVE, F32))

    def mixing(block, state):
        total, mixed = state
        at = pl.ds(pl.multiple_of(block * STEP, STEP), STEP)
        scores = kept[pl.ds(pl.multiple_of((block - first) * STEP, STEP), STEP), :]
        weights = jnp.exp(scores - top)
        total = total + jnp.sum(weights, axis=0, keepdims=True)
        return total, mixed + dot(values[at, :], weights.astype(BF16), TN)

    total, mixed = lax.fori_loop(
        first,
        diagonal + 1,
        mixing,
        (jnp.zeros(place.shape, F32), jnp.zeros((LANES, place.shape[1]), F32)),
    )
    lse_ref[0] = top + jnp.log(total)
    tile = unstack_heads((mixed / total).T)
    mix_ref[...] = tile
    for s in range(STEP // ROWS):
        out_ref[s] = tile[s * ROWS : (s + 1) * ROWS].astype(BF16)


def attend(half, heads, peer, place):
    steps = HALF // STEP
    per_step = STEP // ROWS
    return pl.pallas_call(
        attend_kernel,
        grid_spec=pltpu.PrefetchScalarGridSpec(
            num_scalar_prefetch=1,
            grid=(steps,),
            in_specs=[
                whole((Z, ROWS, 2 * LANES)),
                whole((HALF, LANES)),
                pl.BlockSpec((1, 1, 2 * STEP), lambda i, half: (i, 0, 0)),
            ],
            out_specs=[
                pl.BlockSpec((STEP, LANES), lambda i, half: (i, 0)),
                pl.BlockSpec((per_step, ROWS, LANES), lambda i, half: (i, 0, 0)),
                pl.BlockSpec((1, 1, 2 * STEP), lambda i, half: (i, 0, 0)),
            ],
            scratch_shapes=[
                pltpu.VMEM((2 * HALF, LANES), BF16),
                pltpu.VMEM((2 * HALF, LANES), BF16),
                pltpu.VMEM((HALF + STEP, 2 * STEP), F32),
            ],
        ),
        out_shape=[
            jax.ShapeDtypeStruct((HALF, LANES), F32),
            jax.ShapeDtypeStruct((Z, ROWS, LANES), BF16),
            jax.ShapeDtypeStruct((steps, 1, 2 * STEP), F32),
        ],
        compiler_params=params(),
        cost_estimate=cost(9),
        name="attend",
    )(half, heads, peer, place)


def attend_back_kernel(
    half_ref,
    heads_ref,
    peer_ref,
    place_ref,
    lse_ref,
    dmix_ref,
    mix_ref,
    dq_ref,
    own_ref,
    other_ref,
    keys,
    values,
    dk,
    dv,
):
    i = pl.program_id(0)

    @pl.when(i == 0)
    def _():
        fill_keys(half_ref, heads_ref, peer_ref, keys, values)
        dk[...] = jnp.zeros_like(dk)
        dv[...] = jnp.zeros_like(dv)

    queries = step_queries(heads_ref, i)
    place = place_ref[0]
    lse = lse_ref[0]
    diagonal = half_ref[0] * (HALF // STEP) + i
    first = half_ref[1 + i]
    last = diagonal * STEP + lax.broadcasted_iota(jnp.int32, place.shape, 1) % STEP
    upstream = jnp.concatenate([dmix_ref[s] for s in range(STEP // ROWS)], axis=0).astype(F32)
    delta = jnp.sum(stack_heads(upstream * mix_ref[...]).T, axis=0, keepdims=True)
    upstream = stack_heads(upstream).astype(BF16)

    def step(block, dq):
        at, scores = step_scores(keys, queries, block, place, last)
        probs = jnp.exp(scores - lse)
        probs_grad = dot(values[at, :], upstream, NT)
        scores_grad = (probs * (probs_grad - delta)).astype(BF16)
        dv[at, :] += dot(probs.astype(BF16), upstream)
        dk[at, :] += dot(scores_grad, queries)
        return dq + dot(keys[at, :], scores_grad, TN)

    dq = lax.fori_loop(
        first, diagonal + 1, step, jnp.zeros((LANES, place.shape[1]), F32)
    )
    dq_ref[...] = (unstack_heads(dq.T) * SCALE).astype(BF16)

    @pl.when(i == pl.num_programs(0) - 1)
    def _():
        def joined(at):
            both = [ref[at, :] + pltpu.roll(ref[at, :], 64, 1) for ref in (dk, dv)]
            return jnp.where(lanes_of(both[0]) < 64, *both).astype(BF16)

        own_ref[...] = joined(pl.ds(pl.multiple_of(half_ref[0] * HALF, HALF), HALF))
        other_ref[...] = joined(pl.ds(0, HALF))


def attend_back(half, heads, peer, place, lse, mix_grad, mix):
    steps = HALF // STEP
    per_step = STEP // ROWS
    return pl.pallas_call(
        attend_back_kernel,
        grid_spec=pltpu.PrefetchScalarGridSpec(
            num_scalar_prefetch=1,
            grid=(steps,),
            in_specs=[
                whole((Z, ROWS, 2 * LANES)),
                whole((HALF, LANES)),
                pl.BlockSpec((1, 1, 2 * STEP), lambda i, half: (i, 0, 0)),
                pl.BlockSpec((1, 1, 2 * STEP), lambda i, half: (i, 0, 0)),
                pl.BlockSpec((per_step, ROWS, LANES), lambda i, half: (i, 0, 0)),
                pl.BlockSpec((STEP, LANES), lambda i, half: (i, 0)),
            ],
            out_specs=[
                pl.BlockSpec((STEP, LANES), lambda i, half: (i, 0)),
                whole((HALF, LANES)),
                whole((HALF, LANES)),
            ],
            scratch_shapes=[
                pltpu.VMEM((2 * HALF, LANES), BF16),
                pltpu.VMEM((2 * HALF, LANES), BF16),
                pltpu.VMEM((2 * HALF, LANES), F32),
                pltpu.VMEM((2 * HALF, LANES), F32),
            ],
        ),
        out_shape=[jax.ShapeDtypeStruct((HALF, LANES), BF16)] * 3,
        compiler_params=params(),
        cost_estimate=cost(12),
        name="attend_back",
    )(half, heads, peer, place, lse, mix_grad, mix)


def out_kernel(heads_ref, wout_ref, src_ref, gain_ref, two_ref, res_ref, mix_ref):
    mix = jnp.concatenate([heads_ref[z] for z in range(Z)], axis=1)
    residual = src_ref[...].astype(F32) + dot(mix, wout_ref[...])
    inverse = lax.rsqrt(jnp.mean(residual * residual, axis=1, keepdims=True) + EPSILON)
    mix_ref[...] = mix
    res_ref[...] = residual
    two_ref[...] = (residual * inverse * gain_ref[...]).astype(BF16)


def project_out(heads, out_weight, source, gain):
    rows, width = source.shape
    return pl.pallas_call(
        out_kernel,
        out_shape=[
            jax.ShapeDtypeStruct((rows, width), BF16),
            jax.ShapeDtypeStruct((rows, width), F32),
            jax.ShapeDtypeStruct((rows, width), BF16),
        ],
        compiler_params=params(),
        cost_estimate=cost(3),
        name="project_out",
    )(heads, out_weight, source, gain)


def unpack_kernel(heads_ref, cos_ref, sin_ref, out_ref):
    cos = cos_ref[...]
    sin = -sin_ref[...]
    width = Z * LANES
    for j in range(PAIRS):
        tiles = [heads_ref[2 * j + s].astype(F32) for s in range(2)]
        for s in range(2):
            at = (2 * j + s) * LANES
            out_ref[:, at : at + LANES] = turn(tiles[s][:, :LANES], cos, sin).astype(BF16)
        keys, values = exchange(tiles[0][:, LANES:], tiles[1][:, LANES:])
        at = width + j * LANES
        out_ref[:, at : at + LANES] = turn(keys, cos, sin).astype(BF16)
        at += PAIRS * LANES
        out_ref[:, at : at + LANES] = values.astype(BF16)


def unpack(heads, cos, sin):
    return pl.pallas_call(
        unpack_kernel,
        out_shape=jax.ShapeDtypeStruct((ROWS, 2 * Z * LANES), BF16),
        compiler_params=params(),
        cost_estimate=cost(2.4),
        name="unpack",
    )(heads, cos, sin)


def gather_kernel(c0, c1, c2, c3, wd_ref, a_ref, c_ref, mask_ref):
    @pl.when(pl.program_id(0) == 0)
    def _():
        for i, block in enumerate((c0, c1, c2, c3)):
            rows = slice(i * ROWS, (i + 1) * ROWS)
            c_ref[rows, :] = block[:, : c_ref.shape[1]]
            mask_ref[rows, :] = block[:, c_ref.shape[1] :]

    a_ref[0] = dot(c_ref[...], wd_ref[0], NT).astype(BF16)


def upstream_of_experts(blocks, down_weight):
    experts, hidden, width = down_weight.shape
    rows = 4 * ROWS
    return pl.pallas_call(
        gather_kernel,
        grid=(experts,),
        in_specs=[whole((ROWS, width + LANES))] * 4
        + [pl.BlockSpec((1, hidden, width), lambda e: (e, 0, 0))],
        out_specs=[
            pl.BlockSpec((1, rows, hidden), lambda e: (e, 0, 0)),
            whole((rows, width)),
            whole((rows, LANES)),
        ],
        out_shape=[
            jax.ShapeDtypeStruct((experts, rows, hidden), BF16),
            jax.ShapeDtypeStruct((rows, width), BF16),
            jax.ShapeDtypeStruct((rows, LANES), BF16),
        ],
        compiler_params=params(),
        cost_estimate=cost(6),
        name="upstream_of_experts",
    )(*blocks, down_weight)


def experts_kernel(
    ids_ref,
    x0,
    x1,
    x2,
    x3,
    mask_ref,
    router_ref,
    wg_ref,
    wu_ref,
    a_ref,
    b0,
    b1,
    b2,
    b3,
    x_ref,
    own_gates_ref,
    send_ref,
    own_ref,
    gates,
    dots,
    total,
):
    e = pl.program_id(0)
    width = x_ref.shape[1]

    @pl.when(e == 0)
    def _():
        for i, block in enumerate((x0, x1, x2, x3)):
            x_ref[i * ROWS : (i + 1) * ROWS, :] = block[...]
        logits = dot(x_ref[...], router_ref[...])
        chosen = mask_ref[...].astype(F32) > 0.5
        logits = jnp.where(chosen, logits, NEGATIVE)
        top = jnp.max(logits, axis=1, keepdims=True)
        weights = jnp.where(chosen, jnp.exp(logits - top), 0.0)
        gates[...] = weights / jnp.sum(weights, axis=1, keepdims=True)
        own_gates_ref[...] = gates[:ROWS, :]
        dots[...] = jnp.zeros_like(dots)
        total[...] = jnp.zeros_like(total)

    wg = wg_ref[0]
    wu = wu_ref[0]
    parts = []
    for rows in [slice(r, r + PART) for r in range(0, x_ref.shape[0], PART)]:
        here = lanes_of(gates[rows, :]) == ids_ref[4] + ids_ref[e]
        gate = jnp.sum(jnp.where(here, gates[rows, :], 0.0), axis=1, keepdims=True)
        gate_pre = dot(x_ref[rows, :], wg)
        up_pre = dot(x_ref[rows, :], wu)
        upstream = a_ref[0, rows, :].astype(F32)
        sigmoid = 1.0 / (1.0 + jnp.exp(-gate_pre))
        silu = gate_pre * sigmoid
        acted = silu * up_pre
        gated = upstream * gate
        dots[rows, :] += jnp.where(here, jnp.sum(upstream * acted, axis=1, keepdims=True), 0.0)
        slope = sigmoid + silu * (1.0 - sigmoid)
        gate_pre_grad = (gated * up_pre * slope).astype(BF16)
        up_pre_grad = (gated * silu).astype(BF16)
        parts.append((rows, gate_pre_grad, up_pre_grad, (acted * gate).astype(BF16)))
        total[rows, :] += dot(gate_pre_grad, wg, NT) + dot(up_pre_grad, wu, NT)

    @pl.when(e < 2)
    def _():
        for rows, *values in parts:
            for which, value in enumerate(values):
                send_ref[which, 0, rows, :] = value

    @pl.when(e >= 2)
    def _():
        for rows, *values in parts:
            for which, value in enumerate(values):
                own_ref[which, 0, rows, :] = value

    @pl.when(e == pl.num_programs(0) - 1)
    def _():
        high = dots[...].astype(BF16).astype(F32)
        low = (dots[...] - high).astype(BF16).astype(F32)
        tail = (high + pltpu.roll(low, 16, 1)).astype(BF16)
        for i, out_ref in enumerate((b0, b1, b2, b3)):
            rows = slice(i * ROWS, (i + 1) * ROWS)
            out_ref[:, :width] = total[rows, :].astype(BF16)
            out_ref[:, width:] = tail[rows, :]


def first_two(*block):
    return pl.BlockSpec(block, lambda e, ids: (0, jnp.minimum(e, 1), 0, 0))


def last_two(*block):
    return pl.BlockSpec(block, lambda e, ids: (0, jnp.maximum(e - 2, 0), 0, 0))


def chosen_expert(*block):
    return pl.BlockSpec(block, lambda e, ids: (ids[e], 0, 0))


def experts_main(ids, blocks, mask, router, gate_weight, up_weight, upstream):
    experts, width, hidden = gate_weight.shape
    rows = 4 * ROWS
    return pl.pallas_call(
        experts_kernel,
        grid_spec=pltpu.PrefetchScalarGridSpec(
            num_scalar_prefetch=1,
            grid=(experts,),
            in_specs=[whole((ROWS, width))] * 4
            + [
                whole((rows, LANES)),
                whole((width, LANES)),
                chosen_expert(1, width, hidden),
                chosen_expert(1, width, hidden),
                chosen_expert(1, rows, hidden),
            ],
            out_specs=[whole((ROWS, width + LANES))] * 4
            + [
                whole((rows, width)),
                whole((ROWS, LANES)),
                first_two(3, 1, rows, hidden),
                last_two(3, 1, rows, hidden),
            ],
            scratch_shapes=[
                pltpu.VMEM((rows, LANES), F32),
                pltpu.VMEM((rows, LANES), F32),
                pltpu.VMEM((rows, width), F32),
            ],
        ),
        out_shape=[jax.ShapeDtypeStruct((ROWS, width + LANES), BF16)] * 4
        + [
            jax.ShapeDtypeStruct((rows, width), BF16),
            jax.ShapeDtypeStruct((ROWS, LANES), F32),
            jax.ShapeDtypeStruct((3, 2, rows, hidden), BF16),
            jax.ShapeDtypeStruct((3, 2, rows, hidden), BF16),
        ],
        compiler_params=params(),
        cost_estimate=cost(17),
        name="experts_main",
    )(ids, *blocks, mask, router, gate_weight, up_weight, upstream)


def produce_kernel(ids_ref, send_ref, own_ref, wd_ref, o0, o1, o2, o3, total):
    e = pl.program_id(0)

    @pl.when(e == 0)
    def _():
        total[...] = jnp.zeros_like(total)

    acted = jnp.where(e < 2, send_ref[0, 0], own_ref[0, 0])
    total[...] += dot(acted, wd_ref[0])

    @pl.when(e == pl.num_programs(0) - 1)
    def _():
        for i, out_ref in enumerate((o0, o1, o2, o3)):
            out_ref[...] = total[i * ROWS : (i + 1) * ROWS, :].astype(BF16)


def produce(ids, sent, own, down_weight):
    experts, hidden, width = down_weight.shape
    rows = 4 * ROWS
    return pl.pallas_call(
        produce_kernel,
        grid_spec=pltpu.PrefetchScalarGridSpec(
            num_scalar_prefetch=1,
            grid=(experts,),
            in_specs=[
                pl.BlockSpec((1, 1, rows, hidden), lambda e, ids: (2, jnp.minimum(e, 1), 0, 0)),
                pl.BlockSpec((1, 1, rows, hidden), lambda e, ids: (2, jnp.maximum(e - 2, 0), 0, 0)),
                chosen_expert(1, hidden, width),
            ],
            out_specs=[whole((ROWS, width))] * 4,
            scratch_shapes=[pltpu.VMEM((rows, width), F32)],
        ),
        out_shape=[jax.ShapeDtypeStruct((ROWS, width), BF16)] * 4,
        compiler_params=params(),
        cost_estimate=cost(7),
        name="produce",
    )(ids, sent, own, down_weight)


def store_parts(slots_ref, outs, grad, arrange):
    e = pl.program_id(0)
    rows = grad.shape[0] // 8
    for own in range(2):
        keep_ref, send_ref = outs[2 * own : 2 * own + 2]

        @pl.when(e == own)
        def _():
            for x_lo in range(2):
                for core in range(2):
                    for x_hi in range(2):
                        at = (x_lo * 4 + core * 2 + x_hi) * rows
                        value = arrange(grad[at : at + rows]).astype(BF16)
                        slot = slots_ref[own * 4 + x_hi * 2 + x_lo]

                        @pl.when(slot < 2)
                        def _():
                            keep_ref[slot, core] = value

                        @pl.when(slot >= 2)
                        def _():
                            send_ref[slot - 2, core] = value


def down_grads_kernel(slots_ref, c_ref, co_ref, pack_ref, packo_ref, *outs):
    grad = dot(pack_ref[0, 0], c_ref[...], TN) + dot(packo_ref[0, 0], co_ref[...], TN)

    def arrange(value):
        rows, width = value.shape
        value = value.reshape(Z, rows // Z, width)
        halves = [value[:, :, : width // 2], value[:, :, width // 2 :]]
        return jnp.concatenate(halves, axis=1).reshape(2 * rows, width // 2)

    store_parts(slots_ref, outs, grad, arrange)


def up_grads_kernel(slots_ref, x_ref, xo_ref, pack_ref, packo_ref, *rest):
    outs, xt = rest[:-1], rest[-1]
    half = 4 * ROWS

    @pl.when(pl.program_id(0) == 0)
    def _():
        xt[:, :half] = x_ref[...].T
        xt[:, half:] = xo_ref[...].T

    for which in range(2):
        grad = dot(xt[:, :half], pack_ref[which, 0]) + dot(xt[:, half:], packo_ref[which, 0])
        store_parts(slots_ref, outs[4 * which : 4 * which + 4], grad, lambda value: value)


def expert_grads(kernel, name, slots, tokens, other_tokens, pack, other_pack, scratch, count, first):
    rows, width = tokens.shape
    hidden = pack.shape[3]
    packs = pl.BlockSpec((count, 1, rows, hidden), lambda e, slots: (first, e, 0, 0))
    out = (2, 2, ROWS, hidden)
    outs = pl.pallas_call(
        kernel,
        grid_spec=pltpu.PrefetchScalarGridSpec(
            num_scalar_prefetch=1,
            grid=(2,),
            in_specs=[whole((rows, width))] * 2 + [packs, packs],
            out_specs=[whole(out)] * (4 * count),
            scratch_shapes=scratch,
        ),
        out_shape=[jax.ShapeDtypeStruct(out, BF16)] * (4 * count),
        compiler_params=params(),
        cost_estimate=cost(7 * count - 4),
        name=name,
    )(slots, tokens, other_tokens, pack, other_pack)
    return [
        ((outs[4 * i], outs[4 * i + 2]), (outs[4 * i + 1], outs[4 * i + 3])) for i in range(count)
    ]


def expert_sums_kernel(*refs):
    out_ref = refs[-1]
    for i in range(len(refs) // 3):
        kept, got, last = refs[3 * i : 3 * i + 3]
        total = kept[0].astype(F32) + got[0].astype(F32) + last[...].astype(F32)
        total = total.astype(BF16)
        for core in range(2):
            for z in range(Z):
                out_ref[core, z, i // 2, i % 2] = total[core, z * 16 : (z + 1) * 16]


def expert_sums(parts):
    hidden = parts[0][0][0].shape[3]
    count = len(parts)
    both = pl.BlockSpec((1, 2, ROWS, hidden), lambda i: (0, 0, 0, 0))
    return pl.pallas_call(
        expert_sums_kernel,
        grid=(1,),
        in_specs=[both, both, whole((2, ROWS, hidden))] * (2 * count),
        out_specs=whole((2, Z, count, 2, 16, hidden)),
        out_shape=jax.ShapeDtypeStruct((2, Z, count, 2, 16, hidden), BF16),
        compiler_params=params(),
        cost_estimate=cost(3),
        name="expert_sums",
    )(*[part[e] for parts_of in parts for e in range(2) for part in parts_of])


def dense_kernel(count, with_gain, place_ref, *refs):
    lefts, rights, rest = refs[:count], refs[count : 2 * count], refs[2 * count :]
    parts = [dot(left[...], right[...]) for left, right in zip(lefts, rights)]
    parts = [own + other for own, other in zip(parts[::2], parts[1::2])]
    if with_gain:
        parts[-1] = jnp.where(lanes_of(parts[-1]) == 16, rest[0][...], parts[-1])
        rest = rest[1:]
    for s, out_ref in enumerate(rest):

        @pl.when(pl.program_id(0) == s)
        def _():
            start = 0
            for part in parts:
                out_ref[:, start : start + part.shape[1]] = part.astype(BF16)
                start += part.shape[1]


def dense_part(place, lefts, rights, gain=None):
    total = sum(right.shape[1] for right in rights[::2])

    def of_rows(i, place):
        return place[0] * 4 + (place[1] + i) % 4, 0

    specs = [pl.BlockSpec((ROWS, ROWS), of_rows)] * len(lefts)
    specs += [whole(right.shape) for right in rights]
    operands = [*lefts, *rights]
    if gain is not None:
        specs.append(pl.BlockSpec((ROWS, 1), of_rows))
        operands.append(gain)
    return pl.pallas_call(
        functools.partial(dense_kernel, len(lefts), gain is not None),
        grid_spec=pltpu.PrefetchScalarGridSpec(
            num_scalar_prefetch=1,
            grid=(4,),
            in_specs=specs,
            out_specs=[whole((ROWS, total))] * 4,
        ),
        out_shape=[jax.ShapeDtypeStruct((ROWS, total), BF16)] * 4,
        compiler_params=params(),
        cost_estimate=cost(2),
        name="dense_part",
    )(place, *operands)


def dense_sums_kernel(place_ref, *refs):
    late, early, outs, sums = refs[:4], refs[4:8], refs[8:12], refs[12]
    split = late[0].shape[1]
    for columns, parts in ((slice(0, split), late), (slice(split, sums.shape[1]), early)):
        sums[:, columns] = sum(part[...].astype(F32) for part in parts)
    for s, out_ref in enumerate(outs):
        start = ((place_ref[0] + s) % 4) * 32
        out_ref[...] = sums[pl.ds(pl.multiple_of(start, 32), 32), :].astype(BF16)


def dense_sums(place, late, early):
    total = late[0].shape[1] + early[0].shape[1]
    return pl.pallas_call(
        dense_sums_kernel,
        in_specs=[pl.BlockSpec(memory_space=pltpu.SMEM)]
        + [pl.BlockSpec(memory_space=pltpu.VMEM)] * 8,
        out_shape=[jax.ShapeDtypeStruct((32, total), BF16)] * 4,
        scratch_shapes=[pltpu.VMEM((ROWS, total), F32)],
        compiler_params=params(),
        cost_estimate=cost(3.5),
        name="dense_sums",
    )(place, *late, *early)


def norm_back_kernel(
    b0,
    b1,
    b2,
    b3,
    gates_ref,
    res_ref,
    cot_ref,
    gain_ref,
    router_ref,
    wout_ref,
    res_grad_ref,
    attn_ref,
    dmix_ref,
    gain_grad_ref,
    logits_ref,
):
    width = res_ref.shape[1]
    routed = b0[:, :width].astype(F32)
    tail = b0[:, width:].astype(F32)
    for ref in (b1, b2, b3):
        routed += ref[:, :width].astype(F32)
        tail += ref[:, width:].astype(F32)
    dots = tail + pltpu.roll(tail, LANES - 16, 1)
    gates = gates_ref[...]
    logits_grad = gates * (dots - jnp.sum(gates * dots, axis=1, keepdims=True))
    logits_ref[...] = logits_grad.astype(BF16)
    high = logits_grad.astype(BF16)
    low = (logits_grad - high.astype(F32)).astype(BF16)
    routed += dot(high, router_ref[...], NT) + dot(low, router_ref[...], NT)
    residual = res_ref[...]
    inverse = lax.rsqrt(jnp.mean(residual * residual, axis=1, keepdims=True) + EPSILON)
    normal = residual * inverse
    scaled = routed * gain_ref[...]
    gain_grad_ref[...] = jnp.sum(routed * normal, axis=0, keepdims=True)
    grad = cot_ref[...].astype(F32) + inverse * (
        scaled - normal * jnp.mean(normal * scaled, axis=1, keepdims=True)
    )
    res_grad_ref[...] = grad
    attn_ref[...] = grad.astype(BF16)
    mix_grad = dot(grad.astype(BF16), wout_ref[...], NT).astype(BF16)
    for z in range(Z):
        dmix_ref[z] = mix_grad[:, z * LANES : (z + 1) * LANES]


def norm_two_back(backs, gates, residual, cotangent, gain, router, out_weight):
    rows, width = residual.shape
    return pl.pallas_call(
        norm_back_kernel,
        out_shape=[
            jax.ShapeDtypeStruct((rows, width), F32),
            jax.ShapeDtypeStruct((rows, width), BF16),
            jax.ShapeDtypeStruct((Z, rows, LANES), BF16),
            jax.ShapeDtypeStruct((1, width), F32),
            jax.ShapeDtypeStruct((rows, LANES), BF16),
        ],
        compiler_params=params(),
        cost_estimate=cost(4),
        name="norm_two_back",
    )(*backs, gates, residual, cotangent, gain, router, out_weight)


def send(value, axis, pairs):
    return lax.ppermute(value, axis, pairs)


ACROSS = [(c, c + 8) for c in range(8)]
BACK_ACROSS = [(c + 8, c) for c in range(8)]


def add(*values):
    return sum(value.astype(F32) for value in values)


def from_peers(value):
    return [value] + [send(value, "expert", y_shift(-s)) for s in (1, 2, 3)]


def to_peers(values):
    return [values[0]] + [send(values[s], "expert", y_shift(s)) for s in (1, 2, 3)]


def y_shift(steps):
    return [(i, (i + steps) % 4) for i in range(4)]


def x_shift(steps):
    pairs = []
    for d in range(4):
        for c in range(16):
            x = (c // 8) * 2 + d // 2
            to = (x + steps) % 4
            pairs.append((d * 16 + c, ((to % 2) * 2 + d % 2) * 16 + (to // 2) * 8 + c % 8))
    return pairs


def x_flip(mask):
    pairs = []
    for d in range(4):
        for c in range(16):
            x = (c // 8) * 2 + d // 2
            to = x ^ mask
            pairs.append((d * 16 + c, ((to % 2) * 2 + d % 2) * 16 + (to // 2) * 8 + c % 8))
    return pairs


FLIP_LOW = x_flip(1)
FLIP_BOTH = x_flip(3)
CORE_SWAP = [(d, d ^ 1) for d in range(4)]
CHIPS_Z = [
    [(x_lo * 2 + core) * 16 + x_hi * 8 + z for core in range(2) for z in range(8)]
    for x_lo in range(2)
    for x_hi in range(2)
]
Z_GROUPS = [list(range(8)), list(range(8, 16))]


def swap_z(value):
    return lax.all_to_all(
        value, "context", split_axis=0, concat_axis=0, tiled=True, axis_index_groups=Z_GROUPS
    )


def sum_scatter_z(value):
    return jnp.sum(swap_z(value).astype(F32), axis=0)


def x_first(sent):
    return (
        send(sent[0], ("dp", "context"), FLIP_LOW),
        send(sent[1], ("dp", "context"), FLIP_BOTH),
    )


def x_second(kept, got):
    pairs = (FLIP_BOTH, FLIP_LOW)
    return tuple(
        send(add(kept[e][1], got[e][1]).astype(BF16), ("dp", "context"), pairs[e])
        for e in range(2)
    )


def sum_chips(parts):
    parts = expert_sums(parts)
    _, _, count, _, rows, hidden = parts.shape
    parts = parts.reshape(2 * Z, count * 2 * rows, hidden)
    parts = lax.all_to_all(
        parts, ("dp", "context"), split_axis=0, concat_axis=0, tiled=True, axis_index_groups=CHIPS_Z
    )
    return parts.reshape(2, Z, count, 2, rows, hidden)


def experts_of(parts):
    _, _, count, _, rows, hidden = parts.shape
    total = jnp.sum(parts.astype(F32), axis=1)
    return total.transpose(1, 0, 2, 3, 4).reshape(count, 4, rows, hidden)


def order_matrix(width):
    old = jnp.arange(width, dtype=jnp.int32)
    r, y, z = old % 4, old // 4 % 4, old // 16 % 8
    x_hi, core, x_lo = old // 128 % 2, old // 256 % 2, old // 512
    new = core * 512 + y * 128 + x_hi * 64 + x_lo * 32 + z * 4 + r
    return (jnp.arange(width, dtype=jnp.int32)[:, None] == new[None, :]).astype(BF16)


def on_device(
    inputs,
    cotangent,
    doc_lengths,
    choices,
    first_gain,
    query_weight,
    key_weight,
    value_weight,
    out_weight,
    second_gain,
    router_weight,
    gate_weight,
    up_weight,
    down_weight,
):
    width = inputs.shape[2]
    dp_place = lax.axis_index("dp")
    core = dp_place % 2
    context_place = lax.axis_index("context")
    expert_place = lax.axis_index("expert")
    x_place = context_place // 8 * 2 + dp_place // 2
    own_cot = cotangent[0]

    source = inputs[0].astype(F32)

    starts = jnp.cumsum(doc_lengths[0], dtype=jnp.int32) - doc_lengths[0]

    def begin_of(positions, starts):
        return jnp.max(
            jnp.where(starts[None, :] <= positions[:, None], starts[None, :], 0), axis=1
        )

    positions = context_place * ROWS + jnp.arange(ROWS, dtype=jnp.int32)
    relative = (positions - begin_of(positions, starts)).astype(F32)
    lane = jnp.arange(LANES, dtype=jnp.int32)
    frequency = THETA ** (-(lane % 32).astype(F32) * 2.0 / HEAD_DIM)
    angles = relative[:, None] * frequency[None, :]
    cos = jnp.cos(angles)
    sin = jnp.where(lane % 64 < 32, -1.0, 1.0) * jnp.sin(angles)

    normed_one, heads = project(
        inputs[0], first_gain.reshape(1, width), query_weight, key_weight, value_weight, cos, sin
    )
    doc_lengths, choices, router_weight, second_gain, normed_one = held(
        (doc_lengths, choices, router_weight, second_gain, normed_one)
    )
    starts = jnp.cumsum(doc_lengths[0], dtype=jnp.int32) - doc_lengths[0]
    second = second_gain.reshape(1, width)
    half_at = context_place // Z
    half_positions = half_at * HALF + jnp.arange(HALF, dtype=jnp.int32)
    half_begins = begin_of(half_positions, starts)
    places = (half_positions - half_begins).reshape(HALF // STEP, 1, STEP)
    places = jnp.concatenate([places, places], axis=2)
    half = jnp.concatenate([half_at.reshape(1), half_begins[::STEP] // STEP]).astype(jnp.int32)
    experts = gate_weight.shape[0]
    ids = jnp.concatenate(
        [(jnp.arange(experts) + 2 * (1 - core)) % experts, (expert_place * experts).reshape(1)]
    ).astype(jnp.int32)
    whose = jnp.arange(4)
    flips = (x_place ^ 3, x_place ^ 1)
    slots = jnp.concatenate(
        [
            jnp.where(
                whose == x_place, 0, jnp.where(whose == kept, 1, jnp.where(whose == sent, 2, 3))
            )
            for kept, sent in (flips, flips[::-1])
        ]
    ).astype(jnp.int32)
    own_rows = jnp.stack([core, expert_place]).astype(jnp.int32)
    x_row = x_place.astype(jnp.int32).reshape(1)
    chosen = jnp.any(choices[0][:, :, None] == lane[None, None, :], axis=1).astype(BF16)
    cot_block = jnp.concatenate([own_cot, chosen], axis=1)
    router = jnp.pad(router_weight, ((0, 0), (0, LANES - router_weight.shape[1])))
    order = order_matrix(width)

    heads = swap_z(heads)
    cot_blocks = from_peers(cot_block)
    heads, cot_blocks, half, places = held((heads, cot_blocks, half, places))

    peer = send(heads[:, :, LANES:].reshape(HALF, LANES), "context", ACROSS)
    sorted_one = dot(order, normed_one, NT).astype(BF16)
    other_one = send(sorted_one, "dp", CORE_SWAP)
    peer, sorted_one = held((peer, sorted_one))

    mix_half, mix_heads, lse = attend(half, heads, peer, places)
    mix_heads, cot_blocks = held((mix_heads, cot_blocks))
    mix_heads = swap_z(mix_heads)
    upstream, rows_c, mask = upstream_of_experts(cot_blocks, down_weight)
    other_c = send(rows_c, "dp", CORE_SWAP)
    mix_heads, upstream, rows_c, mask = held((mix_heads, upstream, rows_c, mask))
    normed_two, residual, mix = project_out(mix_heads, out_weight, inputs[0], second)

    x_blocks = from_peers(normed_two)
    sorted_mix = dot(order, mix, NT).astype(BF16)
    sorted_two = dot(order, normed_two, NT).astype(BF16)
    other_mix = send(sorted_mix, "dp", CORE_SWAP)
    other_two = send(sorted_two, "dp", CORE_SWAP)
    x_blocks, sorted_mix, sorted_two = held((x_blocks, sorted_mix, sorted_two))

    *backs, rows_x, gates, pack_sent, pack_own = experts_main(
        ids, x_blocks, mask, router, gate_weight, up_weight, upstream
    )
    backs = to_peers(backs)
    other_pack = send(pack_sent, "dp", CORE_SWAP)
    other_x = send(rows_x, "dp", CORE_SWAP)
    made = produce(ids, pack_sent, pack_own, down_weight)
    backs, made = held((backs, made))

    residual_grad, attn_grad, mix_grad, gain_two_part, logits_grad = norm_two_back(
        backs, gates, residual, own_cot, second, router, out_weight
    )
    rows_x, other_x, pack_own, other_pack, made, mix_grad = held(
        (rows_x, other_x, pack_own, other_pack, made, mix_grad)
    )
    mix_grad = swap_z(mix_grad)
    other_attn = send(attn_grad, "dp", CORE_SWAP)
    other_logits = send(logits_grad, "dp", CORE_SWAP)
    gain_two_part = add(gain_two_part, send(gain_two_part, "dp", CORE_SWAP))
    gain_sorted = (
        gain_two_part.reshape(2, 2, 2, 8, 4, 4).transpose(1, 4, 2, 0, 3, 5).reshape(width, 1)
    )
    (gate_kept, gate_sent), (up_kept, up_sent) = expert_grads(
        up_grads_kernel,
        "up_grads",
        slots,
        rows_x,
        other_x,
        pack_own,
        other_pack,
        [pltpu.VMEM((width, 8 * ROWS), BF16)],
        2,
        0,
    )
    gate_got = x_first(gate_sent)
    made = to_peers(made)
    mix_grad, gate_kept, up_kept, up_sent, other_attn, other_logits, gain_sorted = held(
        (mix_grad, gate_kept, up_kept, up_sent, other_attn, other_logits, gain_sorted)
    )

    dq, dkv, dkv_peer = attend_back(half, heads, peer, places, lse, mix_grad, mix_half)
    dq, dkv, dkv_peer, rows_c, other_c, attn_grad, gate_got = held(
        (dq, dkv, dkv_peer, rows_c, other_c, attn_grad, gate_got)
    )
    dkv_got = send(dkv_peer, "context", BACK_ACROSS)
    ((down_kept, down_sent),) = expert_grads(
        down_grads_kernel, "down_grads", slots, rows_c, other_c, pack_own, other_pack, [], 1, 2
    )
    early = dense_part(
        own_rows,
        (sorted_mix, other_mix, sorted_two, other_two),
        (attn_grad, other_attn, logits_grad, other_logits),
        gain_sorted,
    )
    dkv_got, early, down_kept, down_sent, up_sent, made, gate_got = held(
        (dkv_got, early, down_kept, down_sent, up_sent, made, gate_got)
    )

    dheads = jnp.concatenate([dq, add(dkv, dkv_got).astype(BF16)], axis=1)
    dheads = swap_z(dheads.reshape(Z, ROWS, 2 * LANES))
    early = to_peers(early)
    up_got = x_first(up_sent)
    down_got = x_first(down_sent)
    gate_last = x_second(gate_kept, gate_got)
    dheads, early, up_got, gate_last = held((dheads, early, up_got, gate_last))

    dqkv = unpack(dheads, cos, sin)
    other_dqkv = send(dqkv, "dp", CORE_SWAP)
    late = dense_part(own_rows, (sorted_one, other_one), (dqkv, other_dqkv))
    late, up_kept, down_kept, down_got = held((late, up_kept, down_kept, down_got))
    late = to_peers(late)
    up_last = x_second(up_kept, up_got)
    down_last = x_second(down_kept, down_got)
    gate_sums = sum_chips([(gate_kept, gate_got, gate_last)])
    late, dqkv_held, residual_held, up_last, down_last, gate_sums = held(
        (late, dqkv, residual, up_last, down_last, gate_sums)
    )

    dense = dense_sums(x_row, late, early)
    dense = add(
        dense[0], *[send(dense[s], ("dp", "context"), x_shift(s)) for s in (1, 2, 3)]
    ).astype(BF16)
    sums = sum_chips(
        [
            (up_kept, up_got, up_last),
            (down_kept, down_got, down_last),
        ]
    )
    outputs = (residual_held + add(*made)).astype(BF16)[None]
    half_width = key_weight.shape[1]
    normed_grad = (
        dot(dqkv_held[:, :width], query_weight, NT)
        + dot(dqkv_held[:, width : width + half_width], key_weight, NT)
        + dot(dqkv_held[:, width + half_width :], value_weight, NT)
    )
    inverse_one = lax.rsqrt(jnp.mean(source * source, axis=1, keepdims=True) + EPSILON)
    scaled = normed_grad * first_gain
    grad_inputs = residual_grad + inverse_one * scaled - source * inverse_one**3 * jnp.mean(
        source * scaled, axis=1, keepdims=True
    )
    grad_inputs = grad_inputs.astype(BF16)[None]
    dense, outputs, grad_inputs = held((dense, outputs, grad_inputs))
    dense = jnp.sum(swap_z(dense.reshape(Z, 4, -1)).astype(F32), axis=0)
    grad_gate = experts_of(gate_sums)[0]
    grad_up, grad_down = experts_of(sums)
    hidden = gate_weight.shape[2]
    grad_down = grad_down.reshape(4, 2, 8, hidden).transpose(0, 2, 1, 3).reshape(4, 8, 2 * hidden)
    grad_query = dense[:, :width]
    grad_key = dense[:, width : width + half_width]
    grad_value = dense[:, width + half_width : 2 * width]
    grad_out = dense[:, 2 * width : 3 * width]
    grad_router = dense[:, 3 * width : 3 * width + 16]
    grad_second = dense[:, 3 * width + 16]
    first_row = ((dp_place * 16 + context_place) * 4 + expert_place) * 4

    def rows_of(weight):
        return lax.dynamic_slice_in_dim(weight, first_row, 4, axis=0).astype(F32)

    grad_first = (
        jnp.sum(rows_of(query_weight) * grad_query, axis=1)
        + jnp.sum(rows_of(key_weight) * grad_key, axis=1)
        + jnp.sum(rows_of(value_weight) * grad_value, axis=1)
    ) / lax.dynamic_slice_in_dim(first_gain, first_row, 4, axis=0)
    return (
        outputs,
        grad_inputs,
        grad_first,
        grad_query,
        grad_key,
        grad_value,
        grad_out,
        grad_second,
        grad_router,
        grad_gate,
        grad_up,
        grad_down,
    )


def solution(mesh):
    tokens = P(("dp", "expert"), "context", None)
    rows = P(("dp", "context", "expert"))
    matrix = P(("dp", "context", "expert"), None)
    expert = P("expert", None, None)
    expert_grad = P("expert", ("dp", "context"), None)
    in_specs = (tokens, tokens, P(("dp", "expert"), None), tokens) + (P(),) * 7 + (expert,) * 3
    out_specs = (
        (tokens, tokens, rows)
        + (matrix,) * 4
        + (rows, matrix)
        + (expert_grad,) * 3
    )
    return jax.shard_map(
        on_device, mesh=mesh, in_specs=in_specs, out_specs=out_specs, check_vma=False
    )
```

```python
import functools

import jax
import jax.numpy as jnp
from jax import lax
from jax.experimental import pallas as pl
from jax.experimental.pallas import tpu as pltpu
from jax.sharding import PartitionSpec as P

HEADS = 16
KV_HEADS = 8
HEAD_DIM = 64
TOP = 8
EPSILON = 1e-06
THETA = 10000.0
NEGATIVE = -1e30
SCALE = HEAD_DIM ** (-0.5)
LN2 = 0.6931471805599453
BF16 = jnp.bfloat16
F32 = jnp.float32
ROWS = 128
LANES = 128
Z = 8
HALF = Z * ROWS
STEP = 256
PART = 256
PAIRS = KV_HEADS // 2
VMEM_LIMIT = 60 * 1024 * 1024
SMALL_LIMIT = 32 * 1024 * 1024

NN = (((1,), (0,)), ((), ()))
NT = (((1,), (1,)), ((), ()))
TN = (((0,), (0,)), ((), ()))


def dot(left, right, dims=NN):
    return lax.dot_general(left, right, dims, preferred_element_type=F32)


def lanes_of(value):
    return lax.broadcasted_iota(jnp.int32, value.shape, 1)


def swap_halves(value):
    return jnp.where(
        lanes_of(value) % 64 < 32, pltpu.roll(value, 96, 1), pltpu.roll(value, 32, 1)
    )


def exchange(first, second):
    low = lanes_of(first) < 64
    return (
        jnp.where(low, first, pltpu.roll(second, 64, 1)),
        jnp.where(low, pltpu.roll(first, 64, 1), second),
    )


def stack_heads(tile):
    low = lanes_of(tile) < 64
    return jnp.concatenate([jnp.where(low, tile, 0.0), jnp.where(low, 0.0, tile)], axis=0)


def unstack_heads(stacked):
    rows = stacked.shape[0] // 2
    return jnp.where(lanes_of(stacked[:rows]) < 64, stacked[:rows], stacked[rows:])


def turn(tile, cos, sin):
    return tile * cos + swap_halves(tile) * sin


def params(limit=VMEM_LIMIT):
    return pltpu.CompilerParams(vmem_limit_bytes=limit)


def whole(shape):
    return pl.BlockSpec(shape, lambda *_: (0,) * len(shape))


def column(rows, width):
    return pl.BlockSpec((rows, width), lambda j: (0, j))


def cost(microseconds):
    return pl.CostEstimate(
        flops=int(microseconds * 1.1e9),
        bytes_accessed=int(microseconds * 3.6e6),
        transcendentals=0,
    )


def held(values):
    return lax.optimization_barrier(values)


def project_kernel(
    src_ref, gain_ref, wq_ref, wk_ref, wv_ref, cos_ref, sin_ref, normed_ref, out_ref
):
    @pl.when(pl.program_id(0) == 0)
    def _():
        source = src_ref[...].astype(F32)
        inverse = lax.rsqrt(jnp.mean(source * source, axis=1, keepdims=True) + EPSILON)
        normed_ref[...] = (source * inverse * gain_ref[...]).astype(BF16)

    normed = normed_ref[...]
    cos = cos_ref[...]
    sin = sin_ref[...]
    queries = dot(normed, wq_ref[...])
    keys = turn(dot(normed, wk_ref[...]), cos, sin)
    values = dot(normed, wv_ref[...])
    for which, pair in enumerate(exchange(keys, values)):
        tile = queries[:, which * LANES : (which + 1) * LANES]
        out_ref[which, :, :LANES] = (turn(tile, cos, sin) * (SCALE / LN2)).astype(BF16)
        out_ref[which, :, LANES:] = pair.astype(BF16)


def project(source, gain, query_weight, key_weight, value_weight, cos, sin):
    rows, width = source.shape
    return pl.pallas_call(
        project_kernel,
        grid=(PAIRS,),
        in_specs=[
            whole((rows, width)),
            whole((1, width)),
            column(width, 2 * LANES),
            column(width, LANES),
            column(width, LANES),
            whole((rows, LANES)),
            whole((rows, LANES)),
        ],
        out_specs=[
            whole((rows, width)),
            pl.BlockSpec((2, rows, 2 * LANES), lambda j: (j, 0, 0)),
        ],
        out_shape=[
            jax.ShapeDtypeStruct((rows, width), BF16),
            jax.ShapeDtypeStruct((Z, rows, 2 * LANES), BF16),
        ],
        compiler_params=params(),
        cost_estimate=cost(5),
        name="project",
    )(source, gain, query_weight, key_weight, value_weight, cos, sin)


def fill_keys(half_ref, heads_ref, peer_ref, keys, values):
    own = jnp.concatenate([heads_ref[z, :, LANES:] for z in range(Z)], axis=0)
    for tile, start in ((peer_ref[...], 0), (own, pl.multiple_of(half_ref[0] * HALF, HALF))):
        tile = tile.astype(F32)
        low = lanes_of(tile) < 64
        other = pltpu.roll(tile, 64, 1)
        keys[pl.ds(start, HALF), :] = jnp.where(low, tile, other).astype(BF16)
        values[pl.ds(start, HALF), :] = jnp.where(low, other, tile).astype(BF16)


def step_queries(heads_ref, i):
    tiles = [heads_ref[i * (STEP // ROWS) + s, :, :LANES] for s in range(STEP // ROWS)]
    return stack_heads(jnp.concatenate(tiles, axis=0).astype(F32)).astype(BF16)


def step_scores(keys, queries, block, place, last, masked):
    at = pl.ds(pl.multiple_of(block * STEP, STEP), STEP)
    scores = dot(keys[at, :], queries, NT)
    if masked:
        back = last - (block * STEP + lax.broadcasted_iota(jnp.int32, scores.shape, 0))
        scores = jnp.where((back >= 0) & (back <= place), scores, NEGATIVE)
    return at, scores


def over_blocks(half_ref, i, diagonal, step, state):
    first, inner = half_ref[1 + i], half_ref[1 + HALF // STEP + i]
    state = lax.fori_loop(first, inner, functools.partial(step, True), state)
    state = lax.fori_loop(inner, diagonal, functools.partial(step, False), state)
    return step(True, diagonal, state)


def attend_kernel(
    half_ref, heads_ref, peer_ref, place_ref, mix_ref, out_ref, lse_ref, keys, values, kept
):
    i = pl.program_id(0)

    @pl.when(i == 0)
    def _():
        fill_keys(half_ref, heads_ref, peer_ref, keys, values)

    queries = step_queries(heads_ref, i)
    place = place_ref[0]
    diagonal = half_ref[0] * (HALF // STEP) + i
    first = half_ref[1 + i]
    last = diagonal * STEP + lax.broadcasted_iota(jnp.int32, place.shape, 1) % STEP

    def score(masked, block, top):
        _, scores = step_scores(keys, queries, block, place, last, masked)
        kept[pl.ds(pl.multiple_of((block - first) * STEP, STEP), STEP), :] = scores
        return jnp.maximum(top, jnp.max(scores, axis=0, keepdims=True))

    top = over_blocks(half_ref, i, diagonal, score, jnp.full(place.shape, NEGATIVE, F32))

    def mixing(block, state):
        total, mixed = state
        at = pl.ds(pl.multiple_of(block * STEP, STEP), STEP)
        scores = kept[pl.ds(pl.multiple_of((block - first) * STEP, STEP), STEP), :]
        weights = jnp.exp2(scores - top)
        total = total + jnp.sum(weights, axis=0, keepdims=True)
        return total, mixed + dot(values[at, :], weights.astype(BF16), TN)

    total, mixed = lax.fori_loop(
        first,
        diagonal + 1,
        mixing,
        (jnp.zeros(place.shape, F32), jnp.zeros((LANES, place.shape[1]), F32)),
    )
    lse_ref[0] = top + jnp.log2(total)
    tile = unstack_heads((mixed / total).T)
    mix_ref[...] = tile
    for s in range(STEP // ROWS):
        out_ref[s] = tile[s * ROWS : (s + 1) * ROWS].astype(BF16)


def attend(half, heads, peer, place):
    steps = HALF // STEP
    per_step = STEP // ROWS
    return pl.pallas_call(
        attend_kernel,
        grid_spec=pltpu.PrefetchScalarGridSpec(
            num_scalar_prefetch=1,
            grid=(steps,),
            in_specs=[
                whole((Z, ROWS, 2 * LANES)),
                whole((HALF, LANES)),
                pl.BlockSpec((1, 1, 2 * STEP), lambda i, half: (i, 0, 0)),
            ],
            out_specs=[
                pl.BlockSpec((STEP, LANES), lambda i, half: (i, 0)),
                pl.BlockSpec((per_step, ROWS, LANES), lambda i, half: (i, 0, 0)),
                pl.BlockSpec((1, 1, 2 * STEP), lambda i, half: (i, 0, 0)),
            ],
            scratch_shapes=[
                pltpu.VMEM((2 * HALF, LANES), BF16),
                pltpu.VMEM((2 * HALF, LANES), BF16),
                pltpu.VMEM((HALF + STEP, 2 * STEP), F32),
            ],
        ),
        out_shape=[
            jax.ShapeDtypeStruct((HALF, LANES), F32),
            jax.ShapeDtypeStruct((Z, ROWS, LANES), BF16),
            jax.ShapeDtypeStruct((steps, 1, 2 * STEP), F32),
        ],
        compiler_params=params(),
        cost_estimate=cost(9),
        name="attend",
    )(half, heads, peer, place)


def attend_back_kernel(
    half_ref,
    heads_ref,
    peer_ref,
    place_ref,
    lse_ref,
    dmix_ref,
    mix_ref,
    dq_ref,
    own_ref,
    other_ref,
    keys,
    values,
    dk,
    dv,
):
    i = pl.program_id(0)

    @pl.when(i == 0)
    def _():
        fill_keys(half_ref, heads_ref, peer_ref, keys, values)
        dk[...] = jnp.zeros_like(dk)
        dv[...] = jnp.zeros_like(dv)

    queries = step_queries(heads_ref, i)
    place = place_ref[0]
    lse = lse_ref[0]
    diagonal = half_ref[0] * (HALF // STEP) + i
    last = diagonal * STEP + lax.broadcasted_iota(jnp.int32, place.shape, 1) % STEP
    upstream = jnp.concatenate([dmix_ref[s] for s in range(STEP // ROWS)], axis=0).astype(F32)
    delta = jnp.sum(stack_heads(upstream * mix_ref[...]).T, axis=0, keepdims=True)
    upstream = stack_heads(upstream).astype(BF16)

    def step(masked, block, dq):
        at, scores = step_scores(keys, queries, block, place, last, masked)
        probs = jnp.exp2(scores - lse)
        probs_grad = dot(values[at, :], upstream, NT)
        scores_grad = (probs * (probs_grad - delta)).astype(BF16)
        dv[at, :] += dot(probs.astype(BF16), upstream)
        dk[at, :] += dot(scores_grad, queries)
        return dq + dot(keys[at, :], scores_grad, TN)

    dq = over_blocks(half_ref, i, diagonal, step, jnp.zeros((LANES, place.shape[1]), F32))
    dq_ref[...] = (unstack_heads(dq.T) * SCALE).astype(BF16)

    @pl.when(i == pl.num_programs(0) - 1)
    def _():
        def joined(at):
            both = [ref[at, :] + pltpu.roll(ref[at, :], 64, 1) for ref in (dk, dv)]
            return jnp.where(lanes_of(both[0]) < 64, both[0] * LN2, both[1]).astype(BF16)

        own_ref[...] = joined(pl.ds(pl.multiple_of(half_ref[0] * HALF, HALF), HALF))
        other_ref[...] = joined(pl.ds(0, HALF))


def attend_back(half, heads, peer, place, lse, mix_grad, mix):
    steps = HALF // STEP
    per_step = STEP // ROWS
    return pl.pallas_call(
        attend_back_kernel,
        grid_spec=pltpu.PrefetchScalarGridSpec(
            num_scalar_prefetch=1,
            grid=(steps,),
            in_specs=[
                whole((Z, ROWS, 2 * LANES)),
                whole((HALF, LANES)),
                pl.BlockSpec((1, 1, 2 * STEP), lambda i, half: (i, 0, 0)),
                pl.BlockSpec((1, 1, 2 * STEP), lambda i, half: (i, 0, 0)),
                pl.BlockSpec((per_step, ROWS, LANES), lambda i, half: (i, 0, 0)),
                pl.BlockSpec((STEP, LANES), lambda i, half: (i, 0)),
            ],
            out_specs=[
                pl.BlockSpec((STEP, LANES), lambda i, half: (i, 0)),
                whole((HALF, LANES)),
                whole((HALF, LANES)),
            ],
            scratch_shapes=[
                pltpu.VMEM((2 * HALF, LANES), BF16),
                pltpu.VMEM((2 * HALF, LANES), BF16),
                pltpu.VMEM((2 * HALF, LANES), F32),
                pltpu.VMEM((2 * HALF, LANES), F32),
            ],
        ),
        out_shape=[jax.ShapeDtypeStruct((HALF, LANES), BF16)] * 3,
        compiler_params=params(),
        cost_estimate=cost(12),
        name="attend_back",
    )(half, heads, peer, place, lse, mix_grad, mix)


def out_kernel(heads_ref, wout_ref, src_ref, gain_ref, two_ref, res_ref, mix_ref):
    mix = jnp.concatenate([heads_ref[z] for z in range(Z)], axis=1)
    residual = src_ref[...].astype(F32) + dot(mix, wout_ref[...])
    inverse = lax.rsqrt(jnp.mean(residual * residual, axis=1, keepdims=True) + EPSILON)
    mix_ref[...] = mix
    res_ref[...] = residual
    two_ref[...] = (residual * inverse * gain_ref[...]).astype(BF16)


def project_out(heads, out_weight, source, gain):
    rows, width = source.shape
    return pl.pallas_call(
        out_kernel,
        out_shape=[
            jax.ShapeDtypeStruct((rows, width), BF16),
            jax.ShapeDtypeStruct((rows, width), F32),
            jax.ShapeDtypeStruct((rows, width), BF16),
        ],
        compiler_params=params(SMALL_LIMIT),
        cost_estimate=cost(3),
        name="project_out",
    )(heads, out_weight, source, gain)


def unpack_kernel(heads_ref, cos_ref, sin_ref, out_ref):
    cos = cos_ref[...]
    sin = -sin_ref[...]
    width = Z * LANES
    for j in range(PAIRS):
        tiles = [heads_ref[2 * j + s].astype(F32) for s in range(2)]
        for s in range(2):
            at = (2 * j + s) * LANES
            out_ref[:, at : at + LANES] = turn(tiles[s][:, :LANES], cos, sin).astype(BF16)
        keys, values = exchange(tiles[0][:, LANES:], tiles[1][:, LANES:])
        at = width + j * LANES
        out_ref[:, at : at + LANES] = turn(keys, cos, sin).astype(BF16)
        at += PAIRS * LANES
        out_ref[:, at : at + LANES] = values.astype(BF16)


def unpack(heads, cos, sin):
    return pl.pallas_call(
        unpack_kernel,
        out_shape=jax.ShapeDtypeStruct((ROWS, 2 * Z * LANES), BF16),
        compiler_params=params(),
        cost_estimate=cost(2.4),
        name="unpack",
    )(heads, cos, sin)


def gather_kernel(c0, c1, c2, c3, wd_ref, a_ref, c_ref, mask_ref):
    @pl.when(pl.program_id(0) == 0)
    def _():
        for i, block in enumerate((c0, c1, c2, c3)):
            rows = slice(i * ROWS, (i + 1) * ROWS)
            c_ref[rows, :] = block[:, : c_ref.shape[1]]
            mask_ref[rows, :] = block[:, c_ref.shape[1] :]

    a_ref[0] = dot(c_ref[...], wd_ref[0], NT).astype(BF16)


def upstream_of_experts(blocks, down_weight):
    experts, hidden, width = down_weight.shape
    rows = 4 * ROWS
    return pl.pallas_call(
        gather_kernel,
        grid=(experts,),
        in_specs=[whole((ROWS, width + LANES))] * 4
        + [pl.BlockSpec((1, hidden, width), lambda e: (e, 0, 0))],
        out_specs=[
            pl.BlockSpec((1, rows, hidden), lambda e: (e, 0, 0)),
            whole((rows, width)),
            whole((rows, LANES)),
        ],
        out_shape=[
            jax.ShapeDtypeStruct((experts, rows, hidden), BF16),
            jax.ShapeDtypeStruct((rows, width), BF16),
            jax.ShapeDtypeStruct((rows, LANES), BF16),
        ],
        compiler_params=params(),
        cost_estimate=cost(6),
        name="upstream_of_experts",
    )(*blocks, down_weight)


def experts_kernel(
    ids_ref,
    x0,
    x1,
    x2,
    x3,
    mask_ref,
    router_ref,
    wg_ref,
    wu_ref,
    a_ref,
    b0,
    b1,
    b2,
    b3,
    x_ref,
    own_gates_ref,
    send_ref,
    own_ref,
    gates,
    dots,
    total,
):
    e = pl.program_id(0)
    width = x_ref.shape[1]

    @pl.when(e == 0)
    def _():
        for i, block in enumerate((x0, x1, x2, x3)):
            x_ref[i * ROWS : (i + 1) * ROWS, :] = block[...]
        logits = dot(x_ref[...], router_ref[...])
        chosen = mask_ref[...].astype(F32) > 0.5
        logits = jnp.where(chosen, logits, NEGATIVE)
        top = jnp.max(logits, axis=1, keepdims=True)
        weights = jnp.where(chosen, jnp.exp(logits - top), 0.0)
        gates[...] = weights / jnp.sum(weights, axis=1, keepdims=True)
        own_gates_ref[...] = gates[:ROWS, :]
        dots[...] = jnp.zeros_like(dots)
        total[...] = jnp.zeros_like(total)

    wg = wg_ref[0]
    wu = wu_ref[0]
    parts = []
    for rows in [slice(r, r + PART) for r in range(0, x_ref.shape[0], PART)]:
        here = lanes_of(gates[rows, :]) == ids_ref[4] + ids_ref[e]
        gate = jnp.sum(jnp.where(here, gates[rows, :], 0.0), axis=1, keepdims=True)
        gate_pre = dot(x_ref[rows, :], wg)
        up_pre = dot(x_ref[rows, :], wu)
        upstream = a_ref[0, rows, :].astype(F32)
        sigmoid = 1.0 / (1.0 + jnp.exp(-gate_pre))
        silu = gate_pre * sigmoid
        acted = silu * up_pre
        gated = upstream * gate
        dots[rows, :] += jnp.where(here, jnp.sum(upstream * acted, axis=1, keepdims=True), 0.0)
        slope = sigmoid + silu * (1.0 - sigmoid)
        gate_pre_grad = (gated * up_pre * slope).astype(BF16)
        up_pre_grad = (gated * silu).astype(BF16)
        parts.append((rows, gate_pre_grad, up_pre_grad, (acted * gate).astype(BF16)))
        total[rows, :] += dot(gate_pre_grad, wg, NT) + dot(up_pre_grad, wu, NT)

    @pl.when(e < 2)
    def _():
        for rows, *values in parts:
            for which, value in enumerate(values):
                send_ref[which, 0, rows, :] = value

    @pl.when(e >= 2)
    def _():
        for rows, *values in parts:
            for which, value in enumerate(values):
                own_ref[which, 0, rows, :] = value

    @pl.when(e == pl.num_programs(0) - 1)
    def _():
        high = dots[...].astype(BF16).astype(F32)
        low = (dots[...] - high).astype(BF16).astype(F32)
        tail = (high + pltpu.roll(low, 16, 1)).astype(BF16)
        for i, out_ref in enumerate((b0, b1, b2, b3)):
            rows = slice(i * ROWS, (i + 1) * ROWS)
            out_ref[:, :width] = total[rows, :].astype(BF16)
            out_ref[:, width:] = tail[rows, :]


def first_two(*block):
    return pl.BlockSpec(block, lambda e, ids: (0, jnp.minimum(e, 1), 0, 0))


def last_two(*block):
    return pl.BlockSpec(block, lambda e, ids: (0, jnp.maximum(e - 2, 0), 0, 0))


def chosen_expert(*block):
    return pl.BlockSpec(block, lambda e, ids: (ids[e], 0, 0))


def experts_main(ids, blocks, mask, router, gate_weight, up_weight, upstream):
    experts, width, hidden = gate_weight.shape
    rows = 4 * ROWS
    return pl.pallas_call(
        experts_kernel,
        grid_spec=pltpu.PrefetchScalarGridSpec(
            num_scalar_prefetch=1,
            grid=(experts,),
            in_specs=[whole((ROWS, width))] * 4
            + [
                whole((rows, LANES)),
                whole((width, LANES)),
                chosen_expert(1, width, hidden),
                chosen_expert(1, width, hidden),
                chosen_expert(1, rows, hidden),
            ],
            out_specs=[whole((ROWS, width + LANES))] * 4
            + [
                whole((rows, width)),
                whole((ROWS, LANES)),
                first_two(3, 1, rows, hidden),
                last_two(3, 1, rows, hidden),
            ],
            scratch_shapes=[
                pltpu.VMEM((rows, LANES), F32),
                pltpu.VMEM((rows, LANES), F32),
                pltpu.VMEM((rows, width), F32),
            ],
        ),
        out_shape=[jax.ShapeDtypeStruct((ROWS, width + LANES), BF16)] * 4
        + [
            jax.ShapeDtypeStruct((rows, width), BF16),
            jax.ShapeDtypeStruct((ROWS, LANES), F32),
            jax.ShapeDtypeStruct((3, 2, rows, hidden), BF16),
            jax.ShapeDtypeStruct((3, 2, rows, hidden), BF16),
        ],
        compiler_params=params(),
        cost_estimate=cost(17),
        name="experts_main",
    )(ids, *blocks, mask, router, gate_weight, up_weight, upstream)


def produce_kernel(ids_ref, send_ref, own_ref, wd_ref, o0, o1, o2, o3, total):
    e = pl.program_id(0)

    @pl.when(e == 0)
    def _():
        total[...] = jnp.zeros_like(total)

    acted = jnp.where(e < 2, send_ref[0, 0], own_ref[0, 0])
    total[...] += dot(acted, wd_ref[0])

    @pl.when(e == pl.num_programs(0) - 1)
    def _():
        for i, out_ref in enumerate((o0, o1, o2, o3)):
            out_ref[...] = total[i * ROWS : (i + 1) * ROWS, :].astype(BF16)


def produce(ids, sent, own, down_weight):
    experts, hidden, width = down_weight.shape
    rows = 4 * ROWS
    return pl.pallas_call(
        produce_kernel,
        grid_spec=pltpu.PrefetchScalarGridSpec(
            num_scalar_prefetch=1,
            grid=(experts,),
            in_specs=[
                pl.BlockSpec((1, 1, rows, hidden), lambda e, ids: (2, jnp.minimum(e, 1), 0, 0)),
                pl.BlockSpec((1, 1, rows, hidden), lambda e, ids: (2, jnp.maximum(e - 2, 0), 0, 0)),
                chosen_expert(1, hidden, width),
            ],
            out_specs=[whole((ROWS, width))] * 4,
            scratch_shapes=[pltpu.VMEM((rows, width), F32)],
        ),
        out_shape=[jax.ShapeDtypeStruct((ROWS, width), BF16)] * 4,
        compiler_params=params(),
        cost_estimate=cost(1),
        name="produce",
    )(ids, sent, own, down_weight)


def store_parts(place_ref, outs, grad, arrange, scratch):
    e = pl.program_id(0)
    rows = grad.shape[0] // 8
    scratch[...] = grad
    for own in range(2):

        @pl.when(e == own)
        def _():
            for slot, flip in enumerate((0, 3, 1, 2) if own == 0 else (0, 1, 3, 2)):
                x = place_ref[0] ^ flip
                out_ref = outs[2 * own + slot // 2]
                for core in range(2):
                    at = ((x % 2) * 4 + core * 2 + x // 2) * rows
                    value = scratch[pl.ds(pl.multiple_of(at, rows), rows), :]
                    out_ref[slot % 2, core] = arrange(value).astype(BF16)


def down_grads_kernel(place_ref, c_ref, co_ref, pack_ref, packo_ref, *rest):
    grad = dot(pack_ref[0, 0], c_ref[...], TN) + dot(packo_ref[0, 0], co_ref[...], TN)

    def arrange(value):
        rows, width = value.shape
        value = value.reshape(Z, rows // Z, width)
        halves = [value[:, :, : width // 2], value[:, :, width // 2 :]]
        return jnp.concatenate(halves, axis=1).reshape(2 * rows, width // 2)

    store_parts(place_ref, rest[:4], grad, arrange, rest[4])


def up_grads_kernel(place_ref, x_ref, xo_ref, pack_ref, packo_ref, *rest):
    outs, scratch, xt = rest[:8], rest[8], rest[9]
    half = 4 * ROWS

    @pl.when(pl.program_id(0) == 0)
    def _():
        xt[:, :half] = x_ref[...].T
        xt[:, half:] = xo_ref[...].T

    for which in range(2):
        grad = dot(xt[:, :half], pack_ref[which, 0]) + dot(xt[:, half:], packo_ref[which, 0])
        store_parts(
            place_ref, outs[4 * which : 4 * which + 4], grad, lambda value: value, scratch
        )


def expert_grads(kernel, name, place, tokens, other_tokens, pack, other_pack, scratch, count, first):
    rows, width = tokens.shape
    hidden = pack.shape[3]
    packs = pl.BlockSpec((count, 1, rows, hidden), lambda e, place: (first, e, 0, 0))
    out = (2, 2, ROWS, hidden)
    outs = pl.pallas_call(
        kernel,
        grid_spec=pltpu.PrefetchScalarGridSpec(
            num_scalar_prefetch=1,
            grid=(2,),
            in_specs=[whole((rows, width))] * 2 + [packs, packs],
            out_specs=[whole(out)] * (4 * count),
            scratch_shapes=scratch,
        ),
        out_shape=[jax.ShapeDtypeStruct(out, BF16)] * (4 * count),
        compiler_params=params(),
        cost_estimate=cost(3),
        name=name,
    )(place, tokens, other_tokens, pack, other_pack)
    return [
        ((outs[4 * i], outs[4 * i + 2]), (outs[4 * i + 1], outs[4 * i + 3])) for i in range(count)
    ]


def expert_next_kernel(*refs):
    ins, outs = refs[:-2], refs[-2:]
    for i in range(len(ins) // 2):
        total = ins[2 * i][0].astype(F32) + ins[2 * i + 1][0].astype(F32)
        outs[i % 2][i // 2] = total.astype(BF16)


def expert_next(parts):
    count = len(parts)
    hidden = parts[0][0][0].shape[3]
    out = (count, 2, ROWS, hidden)
    return pl.pallas_call(
        expert_next_kernel,
        grid=(1,),
        in_specs=[pl.BlockSpec((1, 2, ROWS, hidden), lambda i: (1, 0, 0, 0))] * (4 * count),
        out_specs=[whole(out)] * 2,
        out_shape=[jax.ShapeDtypeStruct(out, BF16)] * 2,
        compiler_params=params(),
        cost_estimate=cost(1),
        name="expert_next",
    )(*[part[e] for parts_of in parts for e in range(2) for part in parts_of])


def expert_sums_kernel(*refs):
    ins, lasts, out_ref = refs[:-3], refs[-3:-1], refs[-1]
    for i in range(len(ins) // 2):
        which, e = i // 2, i % 2
        total = ins[2 * i][0].astype(F32) + ins[2 * i + 1][0].astype(F32)
        total = (total + lasts[e][which].astype(F32)).astype(BF16)
        for core in range(2):
            for z in range(Z):
                out_ref[core, z, which, e] = total[core, z * 16 : (z + 1) * 16]


def expert_sums(parts, lasts):
    hidden = parts[0][0][0].shape[3]
    count = len(parts)
    return pl.pallas_call(
        expert_sums_kernel,
        grid=(1,),
        in_specs=[pl.BlockSpec((1, 2, ROWS, hidden), lambda i: (0, 0, 0, 0))] * (4 * count)
        + [whole((count, 2, ROWS, hidden))] * 2,
        out_specs=whole((2, Z, count, 2, 16, hidden)),
        out_shape=jax.ShapeDtypeStruct((2, Z, count, 2, 16, hidden), BF16),
        compiler_params=params(),
        cost_estimate=cost(1),
        name="expert_sums",
    )(*[part[e] for parts_of in parts for e in range(2) for part in parts_of], *lasts)


def dense_kernel(count, with_gain, place_ref, *refs):
    lefts, rights, rest = refs[:count], refs[count : 2 * count], refs[2 * count :]
    parts = [dot(left[...], right[...]) for left, right in zip(lefts, rights)]
    parts = [own + other for own, other in zip(parts[::2], parts[1::2])]
    if with_gain:
        parts[-1] = jnp.where(lanes_of(parts[-1]) == 16, rest[0][...], parts[-1])
        rest = rest[1:]
    for s, out_ref in enumerate(rest):

        @pl.when(pl.program_id(0) == s)
        def _():
            start = 0
            for part in parts:
                out_ref[:, start : start + part.shape[1]] = part.astype(BF16)
                start += part.shape[1]


def dense_part(place, lefts, rights, gain=None):
    total = sum(right.shape[1] for right in rights[::2])

    def of_rows(i, place):
        return place[0] * 4 + (place[1] + i) % 4, 0

    specs = [pl.BlockSpec((ROWS, ROWS), of_rows)] * len(lefts)
    specs += [whole(right.shape) for right in rights]
    operands = [*lefts, *rights]
    if gain is not None:
        specs.append(pl.BlockSpec((ROWS, 1), of_rows))
        operands.append(gain)
    return pl.pallas_call(
        functools.partial(dense_kernel, len(lefts), gain is not None),
        grid_spec=pltpu.PrefetchScalarGridSpec(
            num_scalar_prefetch=1,
            grid=(4,),
            in_specs=specs,
            out_specs=[whole((ROWS, total))] * 4,
        ),
        out_shape=[jax.ShapeDtypeStruct((ROWS, total), BF16)] * 4,
        compiler_params=params(),
        cost_estimate=cost(2),
        name="dense_part",
    )(place, *operands)


def dense_sums_kernel(place_ref, *refs):
    late, early, outs, sums = refs[:4], refs[4:8], refs[8:12], refs[12]
    split = late[0].shape[1]
    for columns, parts in ((slice(0, split), late), (slice(split, sums.shape[1]), early)):
        sums[:, columns] = sum(part[...].astype(F32) for part in parts)
    for s, out_ref in enumerate(outs):
        start = ((place_ref[0] + s) % 4) * 32
        out_ref[...] = sums[pl.ds(pl.multiple_of(start, 32), 32), :].astype(BF16)


def dense_sums(place, late, early):
    total = late[0].shape[1] + early[0].shape[1]
    return pl.pallas_call(
        dense_sums_kernel,
        in_specs=[pl.BlockSpec(memory_space=pltpu.SMEM)]
        + [pl.BlockSpec(memory_space=pltpu.VMEM)] * 8,
        out_shape=[jax.ShapeDtypeStruct((32, total), BF16)] * 4,
        scratch_shapes=[pltpu.VMEM((ROWS, total), F32)],
        compiler_params=params(),
        cost_estimate=cost(2),
        name="dense_sums",
    )(place, *late, *early)


def norm_back_kernel(
    b0,
    b1,
    b2,
    b3,
    gates_ref,
    res_ref,
    cot_ref,
    gain_ref,
    router_ref,
    wout_ref,
    res_grad_ref,
    attn_ref,
    dmix_ref,
    gain_grad_ref,
    logits_ref,
):
    width = res_ref.shape[1]
    routed = b0[:, :width].astype(F32)
    tail = b0[:, width:].astype(F32)
    for ref in (b1, b2, b3):
        routed += ref[:, :width].astype(F32)
        tail += ref[:, width:].astype(F32)
    dots = tail + pltpu.roll(tail, LANES - 16, 1)
    gates = gates_ref[...]
    logits_grad = gates * (dots - jnp.sum(gates * dots, axis=1, keepdims=True))
    logits_ref[...] = logits_grad.astype(BF16)
    high = logits_grad.astype(BF16)
    low = (logits_grad - high.astype(F32)).astype(BF16)
    routed += dot(high, router_ref[...], NT) + dot(low, router_ref[...], NT)
    residual = res_ref[...]
    inverse = lax.rsqrt(jnp.mean(residual * residual, axis=1, keepdims=True) + EPSILON)
    normal = residual * inverse
    scaled = routed * gain_ref[...]
    gain_grad_ref[...] = jnp.sum(routed * normal, axis=0, keepdims=True)
    grad = cot_ref[...].astype(F32) + inverse * (
        scaled - normal * jnp.mean(normal * scaled, axis=1, keepdims=True)
    )
    res_grad_ref[...] = grad
    attn_ref[...] = grad.astype(BF16)
    mix_grad = dot(grad.astype(BF16), wout_ref[...], NT).astype(BF16)
    for z in range(Z):
        dmix_ref[z] = mix_grad[:, z * LANES : (z + 1) * LANES]


def norm_two_back(backs, gates, residual, cotangent, gain, router, out_weight):
    rows, width = residual.shape
    return pl.pallas_call(
        norm_back_kernel,
        out_shape=[
            jax.ShapeDtypeStruct((rows, width), F32),
            jax.ShapeDtypeStruct((rows, width), BF16),
            jax.ShapeDtypeStruct((Z, rows, LANES), BF16),
            jax.ShapeDtypeStruct((1, width), F32),
            jax.ShapeDtypeStruct((rows, LANES), BF16),
        ],
        compiler_params=params(),
        cost_estimate=cost(1),
        name="norm_two_back",
    )(*backs, gates, residual, cotangent, gain, router, out_weight)


def send(value, axis, pairs):
    return lax.ppermute(value, axis, pairs)


ACROSS = [(c, c + 8) for c in range(8)]
BACK_ACROSS = [(c + 8, c) for c in range(8)]


def add(*values):
    return sum(value.astype(F32) for value in values)


def from_peers(value):
    return [value] + [send(value, "expert", y_shift(-s)) for s in (1, 2, 3)]


def to_peers(values):
    return [values[0]] + [send(values[s], "expert", y_shift(s)) for s in (1, 2, 3)]


def y_shift(steps):
    return [(i, (i + steps) % 4) for i in range(4)]


def z_shift(steps):
    return [(c, c // Z * Z + (c + steps) % Z) for c in range(16)]


def x_shift(steps):
    pairs = []
    for d in range(4):
        for c in range(16):
            x = (c // 8) * 2 + d // 2
            to = (x + steps) % 4
            pairs.append((d * 16 + c, ((to % 2) * 2 + d % 2) * 16 + (to // 2) * 8 + c % 8))
    return pairs


def x_flip(mask):
    pairs = []
    for d in range(4):
        for c in range(16):
            to = ((c // 8) * 2 + d // 2) ^ mask
            pairs.append((d * 16 + c, ((to % 2) * 2 + d % 2) * 16 + (to // 2) * 8 + c % 8))
    return pairs


FLIP_LOW = x_flip(1)
FLIP_BOTH = x_flip(3)
CORE_SWAP = [(d, d ^ 1) for d in range(4)]
CHIPS_Z = [
    [(x_lo * 2 + core) * 16 + x_hi * 8 + z for core in range(2) for z in range(8)]
    for x_lo in range(2)
    for x_hi in range(2)
]
Z_GROUPS = [list(range(8)), list(range(8, 16))]


def swap_z(value):
    return lax.all_to_all(
        value, "context", split_axis=0, concat_axis=0, tiled=True, axis_index_groups=Z_GROUPS
    )


def sum_scatter_z(value):
    return jnp.sum(swap_z(value).astype(F32), axis=0)


def x_first(sent):
    return (
        send(sent[0], ("dp", "context"), FLIP_LOW),
        send(sent[1], ("dp", "context"), FLIP_BOTH),
    )


def x_second(low, both):
    return (
        send(low, ("dp", "context"), FLIP_BOTH),
        send(both, ("dp", "context"), FLIP_LOW),
    )


def sum_chips(parts):
    _, _, count, _, rows, hidden = parts.shape
    parts = parts.reshape(2 * Z, count * 2 * rows, hidden)
    parts = lax.all_to_all(
        parts, ("dp", "context"), split_axis=0, concat_axis=0, tiled=True, axis_index_groups=CHIPS_Z
    )
    return parts.reshape(2, Z, count, 2, rows, hidden)


def experts_of(parts):
    _, _, count, _, rows, hidden = parts.shape
    total = jnp.sum(parts.astype(F32), axis=1)
    return total.transpose(1, 0, 2, 3, 4).reshape(count, 4, rows, hidden)


def order_matrix(width):
    old = jnp.arange(width, dtype=jnp.int32)
    r, y, z = old % 4, old // 4 % 4, old // 16 % 8
    x_hi, core, x_lo = old // 128 % 2, old // 256 % 2, old // 512
    new = core * 512 + y * 128 + x_hi * 64 + x_lo * 32 + z * 4 + r
    return (jnp.arange(width, dtype=jnp.int32)[:, None] == new[None, :]).astype(BF16)


def on_device(
    inputs,
    cotangent,
    doc_lengths,
    choices,
    first_gain,
    query_weight,
    key_weight,
    value_weight,
    out_weight,
    second_gain,
    router_weight,
    gate_weight,
    up_weight,
    down_weight,
):
    width = inputs.shape[2]
    dp_place = lax.axis_index("dp")
    core = dp_place % 2
    context_place = lax.axis_index("context")
    expert_place = lax.axis_index("expert")
    x_place = context_place // 8 * 2 + dp_place // 2
    own_cot = cotangent[0]

    source = inputs[0].astype(F32)

    starts = jnp.cumsum(doc_lengths[0], dtype=jnp.int32) - doc_lengths[0]

    def begin_of(positions, starts):
        return jnp.max(
            jnp.where(starts[None, :] <= positions[:, None], starts[None, :], 0), axis=1
        )

    positions = context_place * ROWS + jnp.arange(ROWS, dtype=jnp.int32)
    relative = (positions - begin_of(positions, starts)).astype(F32)
    lane = jnp.arange(LANES, dtype=jnp.int32)
    frequency = THETA ** (-(lane % 32).astype(F32) * 2.0 / HEAD_DIM)
    angles = relative[:, None] * frequency[None, :]
    cos = jnp.cos(angles)
    sin = jnp.where(lane % 64 < 32, -1.0, 1.0) * jnp.sin(angles)

    normed_one, heads = project(
        inputs[0], first_gain.reshape(1, width), query_weight, key_weight, value_weight, cos, sin
    )
    doc_lengths, choices, router_weight, second_gain, normed_one = held(
        (doc_lengths, choices, router_weight, second_gain, normed_one)
    )
    starts = jnp.cumsum(doc_lengths[0], dtype=jnp.int32) - doc_lengths[0]
    second = second_gain.reshape(1, width)
    half_at = context_place // Z
    half_positions = half_at * HALF + jnp.arange(HALF, dtype=jnp.int32)
    half_begins = begin_of(half_positions, starts)
    places = (half_positions - half_begins).reshape(HALF // STEP, 1, STEP)
    places = jnp.concatenate([places, places], axis=2)
    half_first = half_begins[::STEP] // STEP
    half_inner = (half_begins[STEP - 1 :: STEP] + STEP - 1) // STEP
    half_inner = jnp.minimum(half_inner, half_at * (HALF // STEP) + jnp.arange(HALF // STEP))
    half = jnp.concatenate([half_at.reshape(1), half_first, half_inner]).astype(jnp.int32)
    experts = gate_weight.shape[0]
    ids = jnp.concatenate(
        [(jnp.arange(experts) + 2 * (1 - core)) % experts, (expert_place * experts).reshape(1)]
    ).astype(jnp.int32)
    own_rows = jnp.stack([core, expert_place]).astype(jnp.int32)
    x_row = x_place.astype(jnp.int32).reshape(1)
    chosen = jnp.any(choices[0][:, :, None] == lane[None, None, :], axis=1).astype(BF16)
    cot_block = jnp.concatenate([own_cot, chosen], axis=1)
    router = jnp.pad(router_weight, ((0, 0), (0, LANES - router_weight.shape[1])))
    order = order_matrix(width)

    heads = swap_z(heads)
    cot_blocks = from_peers(cot_block)
    heads, cot_blocks, half, places = held((heads, cot_blocks, half, places))

    peer = send(heads[:, :, LANES:].reshape(HALF, LANES), "context", ACROSS)
    sorted_one = dot(order, normed_one, NT).astype(BF16)
    other_one = send(sorted_one, "dp", CORE_SWAP)
    peer, sorted_one = held((peer, sorted_one))

    mix_half, mix_heads, lse = attend(half, heads, peer, places)
    mix_heads, cot_blocks = held((mix_heads, cot_blocks))
    mix_heads = swap_z(mix_heads)
    upstream, rows_c, mask = upstream_of_experts(cot_blocks, down_weight)
    other_c = send(rows_c, "dp", CORE_SWAP)
    mix_heads, upstream, rows_c, mask = held((mix_heads, upstream, rows_c, mask))
    normed_two, residual, mix = project_out(mix_heads, out_weight, inputs[0], second)

    x_blocks = from_peers(normed_two)
    sorted_mix = dot(order, mix, NT).astype(BF16)
    sorted_two = dot(order, normed_two, NT).astype(BF16)
    other_mix = send(sorted_mix, "dp", CORE_SWAP)
    other_two = send(sorted_two, "dp", CORE_SWAP)
    x_blocks, sorted_mix, sorted_two = held((x_blocks, sorted_mix, sorted_two))

    *backs, rows_x, gates, pack_sent, pack_own = experts_main(
        ids, x_blocks, mask, router, gate_weight, up_weight, upstream
    )
    backs = to_peers(backs)
    other_pack = send(pack_sent, "dp", CORE_SWAP)
    other_x = send(rows_x, "dp", CORE_SWAP)
    ((down_kept, down_sent),) = expert_grads(
        down_grads_kernel,
        "down_grads",
        x_row,
        rows_c,
        other_c,
        pack_own,
        other_pack,
        [pltpu.VMEM((gate_weight.shape[2], width), F32)],
        1,
        2,
    )
    backs, down_kept, down_sent = held((backs, down_kept, down_sent))

    residual_grad, attn_grad, mix_grad, gain_two_part, logits_grad = norm_two_back(
        backs, gates, residual, own_cot, second, router, out_weight
    )
    rows_x, other_x, pack_own, other_pack, down_sent, mix_grad = held(
        (rows_x, other_x, pack_own, other_pack, down_sent, mix_grad)
    )
    mix_grad = swap_z(mix_grad)
    down_got = x_first(down_sent)
    (gate_kept, gate_sent), (up_kept, up_sent) = expert_grads(
        up_grads_kernel,
        "up_grads",
        x_row,
        rows_x,
        other_x,
        pack_own,
        other_pack,
        [pltpu.VMEM((width, gate_weight.shape[2]), F32), pltpu.VMEM((width, 8 * ROWS), BF16)],
        2,
        0,
    )
    mix_grad, gate_sent, up_kept, down_got, attn_grad, logits_grad, gain_two_part = held(
        (mix_grad, gate_sent, up_kept, down_got, attn_grad, logits_grad, gain_two_part)
    )
    gate_got = x_first(gate_sent)
    other_attn = send(attn_grad, "dp", CORE_SWAP)
    other_logits = send(logits_grad, "dp", CORE_SWAP)
    other_gain = send(gain_two_part, "dp", CORE_SWAP)

    dq, dkv, dkv_peer = attend_back(half, heads, peer, places, lse, mix_grad, mix_half)
    dq, dkv, dkv_peer, gate_got, other_attn, other_logits, other_gain = held(
        (dq, dkv, dkv_peer, gate_got, other_attn, other_logits, other_gain)
    )
    dkv_got = send(dkv_peer, "context", BACK_ACROSS)
    gain_sorted = add(gain_two_part, other_gain).reshape(2, 2, 2, 8, 4, 4)
    gain_sorted = gain_sorted.transpose(1, 4, 2, 0, 3, 5).reshape(width, 1)
    early = dense_part(
        own_rows,
        (sorted_mix, other_mix, sorted_two, other_two),
        (attn_grad, other_attn, logits_grad, other_logits),
        gain_sorted,
    )
    dkv_got, early, up_sent = held((dkv_got, early, up_sent))

    dheads = jnp.concatenate([dq, add(dkv, dkv_got).astype(BF16)], axis=1)
    dheads = swap_z(dheads.reshape(Z, ROWS, 2 * LANES))
    up_got = x_first(up_sent)
    early = to_peers(early)
    parts = [(gate_kept, gate_got), (up_kept, up_got), (down_kept, down_got)]
    nexts = expert_next(parts)
    dheads, early, nexts = held((dheads, early, nexts))

    dqkv = unpack(dheads, cos, sin)
    other_dqkv = send(dqkv, "dp", CORE_SWAP)
    lasts = x_second(*nexts)
    late = dense_part(own_rows, (sorted_one, other_one), (dqkv, other_dqkv))
    late, pack_sent, pack_own, parts = held((late, pack_sent, pack_own, parts))
    late = to_peers(late)
    made = produce(ids, pack_sent, pack_own, down_weight)
    sums = sum_chips(expert_sums(parts, lasts))
    late, made = held((late, made))

    dense = dense_sums(x_row, late, early)
    dense = [dense[0], *[send(dense[s], ("dp", "context"), x_shift(s)) for s in (1, 2, 3)]]
    dense, sums, made = held((dense, sums, made))
    dense = add(*dense).astype(BF16)
    made = to_peers(made)
    dense = dense.reshape(Z, 4, -1)
    z_place = context_place % Z
    for mask in (1, 2, 4):
        dense = dense.reshape((-1, 2) + dense.shape[1:])
        bit = z_place // mask % 2
        got = send(
            lax.dynamic_index_in_dim(dense, 1 - bit, 1, keepdims=False),
            "context",
            [(c, c ^ mask) for c in range(16)],
        )
        dense = add(lax.dynamic_index_in_dim(dense, bit, 1, keepdims=False), got)
        if mask < 4:
            dense = dense.astype(BF16)
        if mask == 1:
            dense, residual_held, dqkv_held = held((dense, residual, dqkv))
    dense = dense[0]
    half_width = key_weight.shape[1]
    normed_grad = (
        dot(dqkv_held[:, :width], query_weight, NT)
        + dot(dqkv_held[:, width : width + half_width], key_weight, NT)
        + dot(dqkv_held[:, width + half_width :], value_weight, NT)
    )
    inverse_one = lax.rsqrt(jnp.mean(source * source, axis=1, keepdims=True) + EPSILON)
    scaled = normed_grad * first_gain
    grad_inputs = residual_grad + inverse_one * scaled - source * inverse_one**3 * jnp.mean(
        source * scaled, axis=1, keepdims=True
    )
    grad_inputs = grad_inputs.astype(BF16)[None]
    outputs = (residual_held + add(*made)).astype(BF16)[None]
    grad_gate, grad_up, grad_down = experts_of(sums)
    hidden = gate_weight.shape[2]
    grad_down = grad_down.reshape(4, 2, 8, hidden).transpose(0, 2, 1, 3).reshape(4, 8, 2 * hidden)
    grad_query = dense[:, :width]
    grad_key = dense[:, width : width + half_width]
    grad_value = dense[:, width + half_width : 2 * width]
    grad_out = dense[:, 2 * width : 3 * width]
    grad_router = dense[:, 3 * width : 3 * width + 16]
    grad_second = dense[:, 3 * width + 16]
    first_row = ((dp_place * 16 + context_place) * 4 + expert_place) * 4

    def rows_of(weight):
        return lax.dynamic_slice_in_dim(weight, first_row, 4, axis=0).astype(F32)

    grad_first = (
        jnp.sum(rows_of(query_weight) * grad_query, axis=1)
        + jnp.sum(rows_of(key_weight) * grad_key, axis=1)
        + jnp.sum(rows_of(value_weight) * grad_value, axis=1)
    ) / lax.dynamic_slice_in_dim(first_gain, first_row, 4, axis=0)
    return (
        outputs,
        grad_inputs,
        grad_first,
        grad_query,
        grad_key,
        grad_value,
        grad_out,
        grad_second,
        grad_router,
        grad_gate,
        grad_up,
        grad_down,
    )


def solution(mesh):
    tokens = P(("dp", "expert"), "context", None)
    rows = P(("dp", "context", "expert"))
    matrix = P(("dp", "context", "expert"), None)
    expert = P("expert", None, None)
    expert_grad = P("expert", ("dp", "context"), None)
    in_specs = (tokens, tokens, P(("dp", "expert"), None), tokens) + (P(),) * 7 + (expert,) * 3
    out_specs = (
        (tokens, tokens, rows)
        + (matrix,) * 4
        + (rows, matrix)
        + (expert_grad,) * 3
    )
    return jax.shard_map(
        on_device, mesh=mesh, in_specs=in_specs, out_specs=out_specs, check_vma=False
    )
```
